128 devices in a mesh: ctx: 16 (over y_lo, z, core), ep: 8 (over x, y_hi).
Axes of the slice: x: 4, y: 4 (y_hi: 2, y_lo: 2; y = y_hi * 2 + y_lo), z: 4, core: 2. Of those that a mesh axis runs over, the one named last changes fastest.
Arguments:
- stream: bfloat16 [4096, 4096], P('ctx', 'ep'), may hold values from -6 to 6
- queries: bfloat16 [4096, 4096], P('ctx', 'ep'), may hold values from -32 to 32
- keys: bfloat16 [4096, 512], P('ctx'), may hold values from -6 to 6
- values: bfloat16 [4096, 512], P('ctx'), may hold values from -24 to 24
- out_weight: bfloat16 [4096, 4096], P('ep'), may hold values from -0.09375 to 0.09375
- norm_gain: float32 [4096], replicated, may hold values from 0.1 to 1.9
- routes: int32 [4096, 8], P(('ctx', 'ep')), may hold values from 0 to 127, all different within a row; in each aligned block of 32 rows (0 to 31, 32 to 63, ...) at most 3 rows name the same one
- gates: float32 [4096, 8], P(('ctx', 'ep')), may hold values from 0.1 to 1
- w_gate: bfloat16 [128, 4096, 768], P(('ctx', 'ep')), may hold values from -0.09375 to 0.09375
- w_up: bfloat16 [128, 4096, 768], P(('ctx', 'ep')), may hold values from -0.09375 to 0.09375
- w_down: bfloat16 [128, 768, 4096], P(('ctx', 'ep')), may hold values from -0.21875 to 0.21875
Outputs:
- resid: bfloat16 [4096, 4096], P(('ctx', 'ep'))
- expert_sum: bfloat16 [4096, 4096], P(('ctx', 'ep'))
The draws below stay inside these ranges and needn't reach their ends.
Inputs may be any that keep to these rules, and one draw needn't show every extreme that they name: `routes`: in the rows of one device in the expert section (32 positions of the order of the sequence) no expert is named more than 3 times; some expert is named exactly 3 times there.
All inputs are finite; a program needn't handle non-finite values.
Results may differ from the reference program's by a relative error of at most 0.024.
Values may be sent and summed in bfloat16 or wider, within the bound.
A program may use at most 128 MiB of HBM per device.

```python
import math
import jax
import jax.numpy as jnp
import numpy as np
from jax import lax

D = 4096
HD = 128
KVH = 4
QH = 32
FH = 768
TOP = 8
TOKENS = 4096
TOK_EP = 32
EXPERTS = 128
CAP = 3
N_CTX = 16
N_EP = 8


def draw_keys(key, part):
    key = jax.random.fold_in(key, 11)
    base = jnp.clip(jax.random.normal(key, (TOKENS, KVH * HD), jnp.float32), -6.0, 6.0)
    return base.astype(jnp.bfloat16)


def draw_queries(key, part):
    key = jax.random.fold_in(key, 12)
    base = jnp.clip(1.5 * jax.random.normal(key, (TOKENS, QH * HD), jnp.float32), -9.0, 9.0)
    return base.astype(jnp.bfloat16)


def steps_of(own_key, dims, shards, low, top_value):
    def one(axis_at, blocks):
        heights = jax.random.uniform(jax.random.fold_in(jax.random.fold_in(own_key, 6), axis_at), (blocks,), jnp.float32, low / len(shards), top_value / len(shards))
        return jnp.repeat(jnp.exp(heights), dims[axis_at] // blocks).reshape((-1,) + (1,) * (len(dims) - axis_at - 1))

    factor_of = one(*shards[0])
    for cut in shards[1:]:
        factor_of = factor_of * one(*cut)
    return factor_of


def deal_out(rng, own, number, rows, count, top, reach, skew):
    ranking = jax.random.permutation(rng, count)
    packed, usual = load_shares(count, rows * top, reach, skew, True), load_shares(count, rows * top, reach, skew, False)
    places = jnp.arange(count)

    def named(tallies, rotation):
        used = int((tallies > 0).sum())
        fixed = max(1, used // 4)
        moved = fixed + (places - fixed + rotation * (used - fixed)) % max(1, count - fixed)
        return jnp.zeros((count,), jnp.int32).at[ranking[jnp.where(places < fixed, places, moved)]].set(jnp.asarray(tallies, jnp.int32))

    tallies = jnp.where(number % 4 == 0, named(packed, number // 4), named(usual, number - number // 4 - 1))
    mixed = jax.random.permutation(jax.random.fold_in(own, 3), count)
    source_of, receiver = mixed[0:count // 2 * 2:2], mixed[1:count // 2 * 2:2]
    room = jnp.minimum(tallies[source_of] - 1, reach - tallies[receiver]) // 2
    room = jnp.where((source_of == ranking[0]) | (receiver == ranking[0]) | (tallies[receiver] == 0), 0, jnp.maximum(room, 0))
    moved = jax.random.randint(jax.random.fold_in(own, 4), (count // 2,), 0, 1 << 20) % (room + 1)
    tallies = tallies.at[source_of].add(-moved).at[receiver].add(moved)
    members = jnp.searchsorted(jnp.cumsum(tallies), jnp.arange(rows * top), side="right").astype(jnp.int32)
    table = members.reshape(top, rows).T
    table = table[jax.random.permutation(jax.random.fold_in(own, 1), rows)]
    rotation = jax.random.randint(jax.random.fold_in(own, 2), (rows, 1), 0, top)
    return jnp.take_along_axis(table, (jnp.arange(top)[None, :] + rotation) % top, axis=1)


def load_shares(count, total, reach, skew, full):
    weights = [(1 << 20) // math.isqrt(rank ** skew) + 1 for rank in range(1, count + 1)]
    largest = reach if full else min(reach, max(-(-total // count), total * weights[0] // sum(weights)))
    least = 1 if total - largest >= count - 1 else 0
    given, surplus = [largest] + [least] * (count - 1), total - largest - least * (count - 1)
    while surplus > 0:
        candidates = [i for i in range(1, count) if given[i] < largest] or [i for i in range(1, count) if given[i] < reach]
        whole, remaining = sum([weights[i] for i in candidates]), surplus
        for i in candidates:
            more = min(reach - given[i], max(1, remaining * weights[i] // whole), surplus)
            given[i] = given[i] + more
            surplus = surplus - more
    return np.array(given)


def scatter_about(stream_key, extent, spread, reach, cuts=(), kind=jnp.bfloat16):
    loudness = steps_of(stream_key, extent, cuts, -0.22, 0.18) if cuts else 1.0
    array = jax.random.normal(stream_key, extent, jnp.float32) * spread * loudness
    return jnp.minimum(jnp.maximum(array, -reach), reach).astype(kind)


def setup_inputs(seed: int = 0) -> dict:
    streams_of = jax.random.split(jax.random.key(seed), 12)
    stream = scatter_about(streams_of[0], (TOKENS, D), 1.0, 6.0, ((0, 16), (1, 8)))
    queries = draw_queries(jax.random.fold_in(streams_of[11], 71), 0)
    keys = draw_keys(jax.random.fold_in(streams_of[11], 71), 0)
    values = scatter_about(streams_of[3], (TOKENS, KVH * HD), 4.0, 24.0, ((0, 16),))
    out_weight = scatter_about(streams_of[4], (QH * HD, D), (QH * HD) ** -0.5, 0.09375, ((0, 8),))
    norm_gain = jnp.clip(1.0 + 0.18 * jax.random.normal(streams_of[5], (D,), jnp.float32), 0.1, 1.9)
    routes_keys = jax.random.split(jax.random.fold_in(streams_of[6], 1), TOKENS // TOK_EP)
    routes_turns = jax.random.permutation(jax.random.fold_in(streams_of[6], 3), TOKENS // TOK_EP)
    routes = jax.vmap(lambda own, number: deal_out(jax.random.fold_in(streams_of[6], 2), own, number, TOK_EP, EXPERTS, TOP, CAP, 2))(routes_keys, routes_turns).reshape((TOKENS, TOP))
    gates = jnp.clip(jnp.exp(math.log(1.0) - 2.3025851 * jax.random.uniform(streams_of[7], (TOKENS, TOP), jnp.float32) ** steps_of(streams_of[7], (TOKENS, TOP), ((0, 128),), -0.2, 0.2)), 0.1, 1.0)
    w_gate = scatter_about(streams_of[8], (EXPERTS, D, FH), D ** -0.5, 0.09375, ((0, 128),))
    w_up = scatter_about(streams_of[9], (EXPERTS, D, FH), D ** -0.5, 0.09375, ((0, 128),))
    w_down = scatter_about(streams_of[10], (EXPERTS, FH, D), FH ** -0.5, 0.21875, ((0, 128),))
    return {"stream": stream, "queries": queries, "keys": keys, "values": values, "out_weight": out_weight, "norm_gain": norm_gain, "routes": routes, "gates": gates, "w_gate": w_gate, "w_up": w_up, "w_down": w_down}


def attend_rows(query_head, key_head, value_head, first):
    score = jnp.dot(query_head, key_head.T, preferred_element_type=jnp.float32) * HD ** (-0.5)
    query_pos = first + jnp.arange(query_head.shape[0], dtype=jnp.int32)
    key_pos = jnp.arange(key_head.shape[0], dtype=jnp.int32)
    allowed = key_pos[None, :] <= query_pos[:, None]
    score = jnp.where(allowed, score, -1e+30)
    top = lax.optimization_barrier(jnp.max(score, axis=-1, keepdims=True))
    weight = jnp.where(allowed, jnp.exp(score - top), 0.0)
    total = lax.optimization_barrier(jnp.sum(weight, axis=-1))
    mixed = jnp.dot(weight.astype(jnp.bfloat16), value_head, preferred_element_type=jnp.float32)
    return (mixed / total[:, None]).astype(jnp.bfloat16)

def reference(stream, queries, keys, values, out_weight, norm_gain, routes, gates, w_gate, w_up, w_down):
    group = QH // KVH
    span = math.gcd(TOKENS, 1024)
    pieces_out = []
    for block in range(TOKENS // span):
        first = block * span
        ending = first + span
        query_rows = queries[first:ending]
        key_rows = keys[:ending]
        value_rows = values[:ending]

        def one_head(head):
            kv_head = head // group
            query_head = lax.dynamic_slice_in_dim(query_rows, (head * HD).astype(jnp.int32), HD, 1)
            key_head = lax.dynamic_slice_in_dim(key_rows, (kv_head * HD).astype(jnp.int32), HD, 1)
            value_head = lax.dynamic_slice_in_dim(value_rows, (kv_head * HD).astype(jnp.int32), HD, 1)
            return attend_rows(query_head, key_head, value_head, first)
        heads_out = lax.map(one_head, jnp.arange(QH, dtype=jnp.int32))
        pieces_out.append(jnp.transpose(heads_out, (1, 0, 2)).reshape(span, QH * HD))
    attn = jnp.concatenate(pieces_out, axis=0)
    resid = (stream.astype(jnp.float32) + jnp.dot(attn, out_weight, preferred_element_type=jnp.float32)).astype(jnp.bfloat16)
    resid_wide = resid.astype(jnp.float32)
    mean_sq = lax.optimization_barrier(jnp.mean(resid_wide * resid_wide, axis=-1, keepdims=True))
    normed = (resid_wide * lax.rsqrt(mean_sq + 1e-06) * norm_gain[None, :]).astype(jnp.bfloat16)
    flat_routes = routes.reshape(-1)
    flat_gates = gates.reshape(-1)
    token_of = jnp.arange(TOKENS * TOP, dtype=jnp.int32) // TOP
    limit = N_CTX * N_EP * CAP

    def one_expert(carry, pieces):
        gate_mat, up_mat, down_mat, expert = pieces
        chosen = flat_routes == expert
        count = jnp.sum(chosen.astype(jnp.int32))
        picks = jnp.nonzero(chosen, size=limit, fill_value=0)[0].astype(jnp.int32)
        valid = jnp.arange(limit, dtype=jnp.int32) < count
        tokens_here = token_of[picks]
        rows = normed[tokens_here]
        gate_val = jnp.dot(rows, gate_mat, preferred_element_type=jnp.float32)
        up_val = jnp.dot(rows, up_mat, preferred_element_type=jnp.float32)
        hidden = (jax.nn.silu(gate_val) * up_val).astype(jnp.bfloat16)
        answer = jnp.dot(hidden, down_mat, preferred_element_type=jnp.float32).astype(jnp.bfloat16)
        factor = jnp.where(valid, flat_gates[picks], 0.0)
        carry = carry.at[tokens_here].add(factor[:, None] * answer.astype(jnp.float32))
        return (carry, None)
    start = jnp.zeros((TOKENS, D), jnp.float32)
    summed, unused = lax.scan(one_expert, start, (w_gate, w_up, w_down, jnp.arange(EXPERTS, dtype=jnp.int32)))
    return (resid, summed.astype(jnp.bfloat16))
```

```python
import functools

import jax
import jax.numpy as jnp
from jax import lax
from jax.experimental import pallas as pl
from jax.experimental.pallas import tpu as pltpu
from jax.sharding import PartitionSpec as P

D = 4096
HD = 128
KVH = 4
QH = 32
TOP = 8
CAP = 3
ROWS = 16
COLS = D // ROWS
LANES = 128
MESH = pl.DeviceIdType.MESH
N_DEV = 128


def shifted(ctx, ep, j, sign):
    core = (ctx + j // 64) % 2
    z = (ctx // 2 + 4 + sign * (j % 4)) % 4
    y_lo = (ctx // 8 + (j // 4) % 2) % 2
    y_hi = (ep + (j // 8) % 2) % 2
    x = (ep // 2 + 4 + sign * ((j // 16) % 4)) % 4
    return y_lo * 8 + z * 2 + core, x * 2 + y_hi


def offset_of(ctx, ep, to_ctx, to_ep):
    core = (to_ctx + ctx) % 2
    z = (to_ctx // 2 + 4 - (ctx // 2) % 4) % 4
    y_lo = (to_ctx // 8 + ctx // 8) % 2
    y_hi = (to_ep + ep) % 2
    x = (to_ep // 2 + 4 - ep // 2) % 4
    return core * 64 + x * 16 + y_hi * 8 + y_lo * 4 + z


def experts_kernel(
    token_ref, place_ref, gate_ref, x_ref, wg_hbm, wu_hbm, wd_hbm, out_ref,
    wg, wu, wd, send, recv, ans, ret, wide, flat, hid,
    w_sem, send_sem, recv_sem, ans_sem, ret_sem,
):
    ctx = lax.axis_index("ctx")
    ep = lax.axis_index("ep")
    loads = [
        pltpu.make_async_copy(src, dst, w_sem.at[i])
        for i, (src, dst) in enumerate(((wg_hbm.at[0], wg), (wu_hbm.at[0], wu), (wd_hbm.at[0], wd)))
    ]
    for load in loads:
        load.start()
    barrier = pltpu.get_barrier_semaphore()

    def greet(j, carry):
        pl.semaphore_signal(barrier, inc=1, device_id=shifted(ctx, ep, j, 1), device_id_type=MESH)
        return carry

    lax.fori_loop(1, N_DEV, greet, 0)
    pl.semaphore_wait(barrier, N_DEV - 1)

    def pack(into, j, to_ctx, to_ep):
        base = (to_ctx * 8 + to_ep) * CAP
        for s in range(CAP):
            into[CAP * j + s] = x_ref[token_ref[base + s]]

    def dispatch(j, carry):
        to = shifted(ctx, ep, j, 1)
        pack(send, j, *to)
        pltpu.make_async_remote_copy(
            src_ref=send.at[pl.ds(CAP * j, CAP)],
            dst_ref=recv.at[pl.ds(CAP * j, CAP)],
            send_sem=send_sem,
            recv_sem=recv_sem.at[j // 64],
            device_id=to,
            device_id_type=MESH,
        ).start()
        return carry

    lax.fori_loop(1, N_DEV, dispatch, 0)
    pack(recv, 0, ctx, ep)

    half = N_DEV // 2
    rows = half * CAP
    for chunk in range(2):
        first = chunk * half
        begin = max(first, 1)
        arrived = recv.at[pl.ds(CAP * begin, CAP * (first + half - begin))]
        pltpu.make_async_copy(arrived, arrived, recv_sem.at[chunk]).wait()

        def flatten(i, carry, first=first):
            part = recv[pl.ds(CAP * first + 16 * i, 16)].reshape(16 * ROWS, COLS).astype(jnp.float32)
            for h in range(2):
                wide[h, pl.ds(0, 16 * ROWS), :] = part[:, h * LANES : (h + 1) * LANES]
            for r in range(ROWS):
                for h in range(2):
                    flat[pl.ds(16 * i, 16), r * COLS + h * LANES : r * COLS + (h + 1) * LANES] = wide[
                        h, pl.ds(r, 16, stride=ROWS), :
                    ].astype(jnp.bfloat16)
            return carry

        lax.fori_loop(0, rows // 16, flatten, 0)
        if chunk == 0:
            loads[0].wait()
            loads[1].wait()

        def up(n, carry):
            cols = pl.ds(pl.multiple_of(n * 256, 256), 256)
            g = jnp.dot(flat[...], wg[:, cols], preferred_element_type=jnp.float32)
            u = jnp.dot(flat[...], wu[:, cols], preferred_element_type=jnp.float32)
            hid[:, cols] = (g / (1.0 + jnp.exp(-g)) * u).astype(jnp.bfloat16)
            return carry

        lax.fori_loop(0, 3, up, 0)
        if chunk == 0:
            loads[2].wait()

        for r in range(ROWS):
            o = jnp.dot(hid[...], wd[:, r * COLS : (r + 1) * COLS], preferred_element_type=jnp.float32)
            for h in range(2):
                wide[h, pl.ds(r, rows, stride=ROWS), :] = o[:, h * LANES : (h + 1) * LANES]

        def reply(i, carry, first=first):
            j = first + i
            for s in range(CAP):
                for h in range(2):
                    ans[CAP * j + s, :, h * LANES : (h + 1) * LANES] = wide[
                        h, pl.ds(pl.multiple_of((CAP * i + s) * ROWS, ROWS), ROWS), :
                    ].astype(jnp.bfloat16)
            return carry

        def send_back(i, carry, first=first):
            j = first + i
            reply(i, carry)
            pltpu.make_async_remote_copy(
                src_ref=ans.at[pl.ds(CAP * j, CAP)],
                dst_ref=ret.at[pl.ds(CAP * j, CAP)],
                send_sem=ans_sem,
                recv_sem=ret_sem,
                device_id=shifted(ctx, ep, j, -1),
                device_id_type=MESH,
            ).start()
            return carry

        if chunk == 0:
            for s in range(CAP):
                for h in range(2):
                    ret[s, :, h * LANES : (h + 1) * LANES] = wide[h, pl.ds(s * ROWS, ROWS), :].astype(jnp.bfloat16)
        lax.fori_loop(begin - first, half, send_back, 0)

    others = ret.at[pl.ds(CAP, CAP * (N_DEV - 1))]
    pltpu.make_async_copy(others, others, ret_sem).wait()

    def combine(t, carry):
        total = jnp.zeros((ROWS, COLS), jnp.float32)
        for k in range(TOP):
            total += gate_ref[t * TOP + k] * ret[place_ref[t * TOP + k]].astype(jnp.float32)
        for h in range(2):
            wide[h, pl.ds(pl.multiple_of(t * ROWS, ROWS), ROWS), :] = total[:, h * LANES : (h + 1) * LANES]
        return carry

    lax.fori_loop(0, 32, combine, 0)
    for r in range(ROWS):
        for h in range(2):
            out_ref[:, r * COLS + h * LANES : r * COLS + (h + 1) * LANES] = wide[
                h, pl.ds(r, 32, stride=ROWS), :
            ].astype(jnp.bfloat16)

    sent = send.at[pl.ds(CAP, CAP * (N_DEV - 1))]
    pltpu.make_async_copy(sent, sent, send_sem).wait()
    answered = ans.at[pl.ds(CAP, CAP * (N_DEV - 1))]
    pltpu.make_async_copy(answered, answered, ans_sem).wait()


def experts(tokens, places, gates, blocks, w_gate, w_up, w_down):
    smem = pl.BlockSpec(memory_space=pltpu.SMEM)
    vmem = pl.BlockSpec(memory_space=pltpu.VMEM)
    hbm = pl.BlockSpec(memory_space=pl.ANY)
    slots = N_DEV * CAP
    hidden = w_gate.shape[2]
    box = pltpu.VMEM((slots, ROWS, COLS), jnp.bfloat16)
    return pl.pallas_call(
        experts_kernel,
        out_shape=jax.ShapeDtypeStruct((32, D), jnp.bfloat16),
        in_specs=[smem, smem, smem, vmem, hbm, hbm, hbm],
        out_specs=vmem,
        scratch_shapes=[
            pltpu.VMEM((D, hidden), jnp.bfloat16),
            pltpu.VMEM((D, hidden), jnp.bfloat16),
            pltpu.VMEM((hidden, D), jnp.bfloat16),
            box, box, box, box,
            pltpu.VMEM((2, slots // 2 * ROWS, LANES), jnp.float32),
            pltpu.VMEM((slots // 2, D), jnp.bfloat16),
            pltpu.VMEM((slots // 2, hidden), jnp.bfloat16),
            pltpu.SemaphoreType.DMA((3,)),
            pltpu.SemaphoreType.DMA,
            pltpu.SemaphoreType.DMA((2,)),
            pltpu.SemaphoreType.DMA,
            pltpu.SemaphoreType.DMA,
        ],
        compiler_params=pltpu.CompilerParams(
            collective_id=1, has_side_effects=True, vmem_limit_bytes=56 * 1024 * 1024
        ),
        name="experts",
    )(tokens, places, gates, blocks, w_gate, w_up, w_down)


def local(
    stream, queries, keys, values, out_weight, norm_gain, routes, gates, w_gate, w_up, w_down
):
    n_ep = lax.axis_size("ep")
    ctx_index = lax.axis_index("ctx")
    ep_index = lax.axis_index("ep")
    rows = queries.shape[0]
    per_dev = queries.shape[1] // HD
    group = QH // KVH

    flat_routes = routes.reshape(-1)
    entries = flat_routes.shape[0]
    order = jnp.arange(entries, dtype=jnp.int32)
    same = (flat_routes[:, None] == flat_routes[None, :]) & (order[None, :] < order[:, None])
    rank = jnp.sum(same.astype(jnp.int32), axis=1)
    slot = flat_routes * CAP + rank
    table = jnp.arange(N_DEV * CAP, dtype=jnp.int32)
    tokens = jnp.sum(jnp.where(slot[None, :] == table[:, None], (order // TOP)[None, :], 0), axis=1)
    places = offset_of(ctx_index, ep_index, flat_routes // n_ep, flat_routes % n_ep) * CAP + rank

    kv_head = ep_index * per_dev // group
    key_own = lax.dynamic_slice_in_dim(keys, kv_head * HD, HD, 1)
    value_own = lax.dynamic_slice_in_dim(values, kv_head * HD, HD, 1)
    query_heads = queries.reshape(rows, per_dev, HD)
    query_pos = ctx_index * rows + jnp.arange(rows, dtype=jnp.int32)
    scale = HD ** (-0.5)
    start_state = (
        jnp.full((per_dev, rows), -1e30, jnp.float32),
        jnp.zeros((per_dev, rows), jnp.float32),
        jnp.zeros((rows, per_dev, HD), jnp.float32),
    )
    carry = start_state
    key_piece = lax.all_gather(key_own, "ctx", axis=0, tiled=True)
    value_piece = lax.all_gather(value_own, "ctx", axis=0, tiled=True)
    count = key_piece.shape[0]
    width = 512
    key_blocks = key_piece.reshape(count // width, width, HD)
    value_blocks = value_piece.reshape(count // width, width, HD)
    offsets = jnp.arange(count // width, dtype=jnp.int32) * width

    def one_block(state, inputs):
        running, total, accum = state
        key_block, value_block, offset = inputs
        key_pos = offset + jnp.arange(width, dtype=jnp.int32)
        score = (
            jnp.einsum("qhd,kd->hqk", query_heads, key_block, preferred_element_type=jnp.float32)
            * scale
        )
        allowed = (key_pos[None, :] <= query_pos[:, None])[None]
        score = jnp.where(allowed, score, -1e30)
        newest = jnp.maximum(running, jnp.max(score, axis=-1))
        weight = jnp.where(allowed, jnp.exp(score - newest[..., None]), 0.0)
        fade = jnp.exp(running - newest)
        total = total * fade + jnp.sum(weight, axis=-1)
        mixed = jnp.einsum(
            "hqk,kd->qhd",
            weight.astype(jnp.bfloat16),
            value_block,
            preferred_element_type=jnp.float32,
        )
        accum = accum * jnp.transpose(fade)[:, :, None] + mixed
        return ((newest, total, accum), None)

    carry, unused = lax.scan(one_block, carry, (key_blocks, value_blocks, offsets))
    running, total, accum = carry
    attn = (
        (accum / jnp.transpose(total)[:, :, None]).astype(jnp.bfloat16).reshape(rows, per_dev * HD)
    )
    projected = jnp.dot(attn, out_weight, preferred_element_type=jnp.float32)
    summed = lax.psum_scatter(
        projected.astype(jnp.bfloat16), "ep", scatter_dimension=1, tiled=True
    ).astype(jnp.float32)
    resid_cols = (summed + stream.astype(jnp.float32)).astype(jnp.bfloat16)
    resid = lax.all_to_all(resid_cols, "ep", split_axis=0, concat_axis=1, tiled=True)
    resid_wide = resid.astype(jnp.float32)
    mean_sq = jnp.mean(resid_wide * resid_wide, axis=-1, keepdims=True)
    normed = (resid_wide * lax.rsqrt(mean_sq + 1e-06) * norm_gain[None, :]).astype(jnp.bfloat16)
    expert_sum = experts(
        tokens, places, gates.reshape(-1), normed.reshape(-1, ROWS, COLS), w_gate, w_up, w_down
    )
    return (resid, expert_sum)


def solution(mesh):
    placed = (
        P("ctx", "ep"),
        P("ctx", "ep"),
        P("ctx", None),
        P("ctx", None),
        P("ep", None),
        P(),
        P(("ctx", "ep"), None),
        P(("ctx", "ep"), None),
        P(("ctx", "ep"), None, None),
        P(("ctx", "ep"), None, None),
        P(("ctx", "ep"), None, None),
    )
    return jax.shard_map(
        local,
        mesh=mesh,
        in_specs=placed,
        out_specs=(P(("ctx", "ep"), None), P(("ctx", "ep"), None)),
        check_vma=False,
    )
```

```python
import functools

import jax
import jax.numpy as jnp
from jax import lax
from jax.experimental import pallas as pl
from jax.experimental.pallas import tpu as pltpu
from jax.sharding import PartitionSpec as P

D = 4096
HD = 128
TOP = 8
CAP = 3
ROWS = 16
COLS = D // ROWS
LANES = 128
MESH = pl.DeviceIdType.MESH
N_DEV = 128


def shifted(ctx, ep, j, sign):
    core = (ctx + j // 64) % 2
    z = (ctx // 2 + 4 + sign * (j % 4)) % 4
    y_lo = (ctx // 8 + (j // 4) % 2) % 2
    y_hi = (ep + (j // 8) % 2) % 2
    x = (ep // 2 + 4 + sign * ((j // 16) % 4)) % 4
    return y_lo * 8 + z * 2 + core, x * 2 + y_hi


def offset_of(ctx, ep, to_ctx, to_ep):
    core = (to_ctx + ctx) % 2
    z = (to_ctx // 2 + 4 - (ctx // 2) % 4) % 4
    y_lo = (to_ctx // 8 + ctx // 8) % 2
    y_hi = (to_ep + ep) % 2
    x = (to_ep // 2 + 4 - ep // 2) % 4
    return core * 64 + x * 16 + y_hi * 8 + y_lo * 4 + z


def kv_peer(ctx, ep, o, sign):
    core = ctx % 2
    y = (ep % 2) * 2 + ctx // 8
    z = (ctx // 2 + 4 + sign * (o % 4)) % 4
    step = (o // 4) * (1 + 2 * core)
    y = (y + 4 + sign * step) % 4
    return (y % 2) * 8 + z * 2 + core, (ep // 2) * 2 + y // 2


def ep_peer(ep, o, sign):
    return ((ep // 2 + 4 + sign * (o // 2)) % 4) * 2 + (ep + o) % 2


def attend_kernel(
    q_ref, k_ref, v_ref, stream_ref, gain_ref, ow_hbm, resid_ref, blocks_ref,
    ow, kall, vall, score, qs, attn, part_out, part_in, stream_in, wide,
    ow_sem, k_send, v_send, k_recv, v_recv, k_sib, v_sib, st_send, st_recv, p_send, p_recv,
):
    ctx = lax.axis_index("ctx")
    ep = lax.axis_index("ep")
    load = pltpu.make_async_copy(ow_hbm, ow, ow_sem)
    load.start()
    sibling = (ctx // 2 * 2 + (ctx + 1) % 2, ep)
    barrier = pltpu.get_barrier_semaphore()
    for o in range(1, 8):
        pl.semaphore_signal(barrier, inc=1, device_id=kv_peer(ctx, ep, o, -1), device_id_type=MESH)
        pl.semaphore_signal(barrier, inc=1, device_id=(ctx, ep_peer(ep, o, -1)), device_id_type=MESH)
    pl.semaphore_signal(barrier, inc=1, device_id=sibling, device_id_type=MESH)

    rows = q_ref.shape[0]

    def block(c):
        return pl.ds(pl.multiple_of(c * rows, rows), rows)

    head = pl.ds(pl.multiple_of(ep // 2 * HD, HD), HD)
    kall[block(ctx), :] = k_ref[:, head]
    vall[block(ctx), :] = v_ref[:, head]
    pl.semaphore_wait(barrier, 15)

    def share(ref, c, send, recv, to):
        return pltpu.make_async_remote_copy(
            src_ref=ref.at[block(c)],
            dst_ref=ref.at[block(c)],
            send_sem=send,
            recv_sem=recv,
            device_id=to,
            device_id_type=MESH,
        )

    for o in (4, 1, 3, 5, 7, 2, 6):
        to = kv_peer(ctx, ep, o, 1)
        share(kall, ctx, k_send, k_recv.at[o], to).start()
        share(vall, ctx, v_send, v_recv.at[o], to).start()
    share(kall, ctx, k_send, k_sib.at[0], sibling).start()
    share(vall, ctx, v_send, v_sib.at[0], sibling).start()

    def landed(ref, c, sem):
        part = ref.at[block(c)]
        pltpu.make_async_copy(part, part, sem).wait()

    for o in (4, 1, 3, 5, 7, 2, 6):
        c = kv_peer(ctx, ep, o, -1)[0]
        landed(kall, c, k_recv.at[o])
        share(kall, c, k_send, k_sib.at[o], sibling).start()
        landed(vall, c, v_recv.at[o])
        share(vall, c, v_send, v_sib.at[o], sibling).start()

    for o in range(1, 8):
        to = ep_peer(ep, o, 1)
        pltpu.make_async_remote_copy(
            src_ref=stream_ref.at[pl.ds(pl.multiple_of(to * 32, 32), 32)],
            dst_ref=stream_in.at[o],
            send_sem=st_send,
            recv_sem=st_recv,
            device_id=(ctx, to),
            device_id_type=MESH,
        ).start()

    for o in range(8):
        c = kv_peer(ctx, ep, o, -1)[0]
        other = c // 2 * 2 + (c + 1) % 2
        landed(kall, other, k_sib.at[o])
        landed(vall, other, v_sib.at[o])
    load.wait()

    width = score.shape[2]
    factor = HD ** (-0.5) * 1.4426950408889634
    heads = q_ref.shape[1] // HD

    def one_part(i, carry):
        dx = (i + 1) % 4
        x = (ep // 2 + dx) % 4
        first = pl.multiple_of(x * 64, 64)
        for h in range(heads):
            qs[64 * h : 64 * h + 64, :] = q_ref[pl.ds(first, 64), HD * h : HD * h + HD]
        last = (ctx * rows + first) // width

        def scores(t):
            keys = kall[pl.ds(pl.multiple_of(t * width, width), width), :]
            return lax.dot_general(
                qs[...], keys, (((1,), (1,)), ((), ())), preferred_element_type=jnp.float32
            )

        def top_of(s, top):
            for j in range(width // LANES):
                top = jnp.maximum(top, s[:, j * LANES : (j + 1) * LANES])
            return top

        def look(t, top):
            s = scores(t)
            score[t] = s
            return top_of(s, top)

        top = lax.fori_loop(0, last, look, jnp.full((64 * heads, LANES), -1e30, jnp.float32))
        s = scores(last)
        query_pos = ctx * rows + first + lax.broadcasted_iota(jnp.int32, s.shape, 0) % 64
        key_pos = last * width + lax.broadcasted_iota(jnp.int32, s.shape, 1)
        s = jnp.where(key_pos <= query_pos, s, -1e30)
        score[last] = s
        top = jnp.max(top_of(s, top), axis=1, keepdims=True)

        def mix(t, state):
            total, mixed = state
            weight = jnp.exp2((score[t] - top) * factor)
            for j in range(width // LANES):
                total = total + weight[:, j * LANES : (j + 1) * LANES]
            mixed = mixed + jnp.dot(
                weight.astype(jnp.bfloat16),
                vall[pl.ds(pl.multiple_of(t * width, width), width), :],
                preferred_element_type=jnp.float32,
            )
            return total, mixed

        zero = jnp.zeros((64 * heads, LANES), jnp.float32)
        total, mixed = lax.fori_loop(0, last + 1, mix, (zero, zero))
        mixed = (mixed / jnp.sum(total, axis=1, keepdims=True)).astype(jnp.bfloat16)
        for h in range(heads):
            attn[:, HD * h : HD * h + HD] = mixed[64 * h : 64 * h + 64, :]

        def project(n, carry):
            cols = pl.ds(pl.multiple_of(n * 512, 512), 512)
            p = jnp.dot(attn[...], ow[:, cols], preferred_element_type=jnp.float32).astype(jnp.bfloat16)
            for y_hi in range(2):
                part_out[2 * dx + (ep + y_hi) % 2, :, cols] = p[32 * y_hi : 32 * y_hi + 32, :]
            return carry

        lax.fori_loop(0, D // 512, project, 0)
        for k in range(2):
            o = 2 * dx + 1 - k

            @pl.when(o > 0)
            def _():
                pltpu.make_async_remote_copy(
                    src_ref=part_out.at[o],
                    dst_ref=part_in.at[o],
                    send_sem=p_send,
                    recv_sem=p_recv,
                    device_id=(ctx, ep_peer(ep, o, 1)),
                    device_id_type=MESH,
                ).start()

        return carry

    lax.fori_loop(0, 4, one_part, 0)

    def all_of(ref, sem):
        part = ref.at[pl.ds(1, 7)]
        pltpu.make_async_copy(part, part, sem).wait()

    all_of(stream_in, st_recv)
    all_of(part_in, p_recv)
    squares = jnp.zeros((32, LANES), jnp.float32)
    for o in range(8):
        source = ep_peer(ep, o, -1)
        cols = pl.ds(pl.multiple_of(source * 512, 512), 512)
        if o == 0:
            own = stream_ref[pl.ds(pl.multiple_of(ep * 32, 32), 32), :]
        else:
            own = stream_in[o]
        total = part_out[0, :, cols].astype(jnp.float32)
        for p in range(1, 8):
            total += part_in[p, :, cols].astype(jnp.float32)
        total = (total + own.astype(jnp.float32)).astype(jnp.bfloat16)
        resid_ref[:, cols] = total
        total = total.astype(jnp.float32)
        for j in range(4):
            piece = total[:, j * LANES : (j + 1) * LANES]
            squares += piece * piece
    inverse = lax.rsqrt(jnp.sum(squares, axis=1, keepdims=True) / D + 1e-06)
    for r in range(ROWS):
        for h in range(2):
            at = r * COLS + h * LANES
            wide[h, pl.ds(r, 32, stride=ROWS), :] = (
                resid_ref[:, at : at + LANES].astype(jnp.float32) * inverse * gain_ref[:, at : at + LANES]
            )

    def store(t, carry):
        for h in range(2):
            blocks_ref[t, :, h * LANES : (h + 1) * LANES] = wide[
                h, pl.ds(pl.multiple_of(t * ROWS, ROWS), ROWS), :
            ].astype(jnp.bfloat16)
        return carry

    lax.fori_loop(0, 32, store, 0)

    for ref, sem in ((kall, k_send), (vall, v_send)):
        sent = ref.at[pl.ds(0, 15 * rows)]
        pltpu.make_async_copy(sent, sent, sem).wait()
    all_of(stream_in, st_send)
    all_of(part_out, p_send)


def attend(queries, keys, values, stream, norm_gain, out_weight):
    vmem = pl.BlockSpec(memory_space=pltpu.VMEM)
    hbm = pl.BlockSpec(memory_space=pl.ANY)
    rows, width = queries.shape
    positions = rows * 16
    bf16, f32 = jnp.bfloat16, jnp.float32
    one = pltpu.SemaphoreType.DMA
    eight = pltpu.SemaphoreType.DMA((8,))
    return pl.pallas_call(
        attend_kernel,
        out_shape=(
            jax.ShapeDtypeStruct((32, D), bf16),
            jax.ShapeDtypeStruct((32, ROWS, COLS), bf16),
        ),
        in_specs=[vmem, vmem, vmem, vmem, vmem, hbm],
        out_specs=(vmem, vmem),
        scratch_shapes=[
            pltpu.VMEM(out_weight.shape, bf16),
            pltpu.VMEM((positions, HD), bf16),
            pltpu.VMEM((positions, HD), bf16),
            pltpu.VMEM((positions // 1024, width // HD * 64, 1024), f32),
            pltpu.VMEM((width // HD * 64, HD), bf16),
            pltpu.VMEM((64, width), bf16),
            pltpu.VMEM((8, 32, D), bf16),
            pltpu.VMEM((8, 32, D), bf16),
            pltpu.VMEM((8, 32, D // 8), bf16),
            pltpu.VMEM((2, 32 * ROWS, LANES), f32),
            one, one, one, eight, eight, eight, eight, one, one, one, one,
        ],
        compiler_params=pltpu.CompilerParams(
            collective_id=0, has_side_effects=True, vmem_limit_bytes=48 * 1024 * 1024
        ),
        name="attend",
    )(queries, keys, values, stream, norm_gain[None, :], out_weight)


def experts_kernel(
    token_ref, place_ref, gate_ref, x_ref, wg_hbm, wu_hbm, wd_hbm, out_ref,
    wg, wu, wd, send, recv, ans, ret, wide, flat, hid,
    w_sem, send_sem, recv_sem, ans_sem, ret_sem,
):
    ctx = lax.axis_index("ctx")
    ep = lax.axis_index("ep")
    loads = [
        pltpu.make_async_copy(src, dst, w_sem.at[i])
        for i, (src, dst) in enumerate(((wg_hbm.at[0], wg), (wu_hbm.at[0], wu), (wd_hbm.at[0], wd)))
    ]
    for load in loads:
        load.start()
    barrier = pltpu.get_barrier_semaphore()

    def greet(j, carry):
        pl.semaphore_signal(barrier, inc=1, device_id=shifted(ctx, ep, j, 1), device_id_type=MESH)
        return carry

    lax.fori_loop(1, N_DEV, greet, 0)
    pl.semaphore_wait(barrier, N_DEV - 1)

    def pack(into, j, to_ctx, to_ep):
        base = (to_ctx * 8 + to_ep) * CAP
        for s in range(CAP):
            into[CAP * j + s] = x_ref[token_ref[base + s]]

    def dispatch(j, carry):
        to = shifted(ctx, ep, j, 1)
        pack(send, j, *to)
        pltpu.make_async_remote_copy(
            src_ref=send.at[pl.ds(CAP * j, CAP)],
            dst_ref=recv.at[pl.ds(CAP * j, CAP)],
            send_sem=send_sem,
            recv_sem=recv_sem.at[j // 64],
            device_id=to,
            device_id_type=MESH,
        ).start()
        return carry

    lax.fori_loop(1, N_DEV, dispatch, 0)
    pack(recv, 0, ctx, ep)

    half = N_DEV // 2
    rows = half * CAP
    for chunk in range(2):
        first = chunk * half
        begin = max(first, 1)
        arrived = recv.at[pl.ds(CAP * begin, CAP * (first + half - begin))]
        pltpu.make_async_copy(arrived, arrived, recv_sem.at[chunk]).wait()

        def flatten(i, carry, first=first):
            part = recv[pl.ds(CAP * first + 16 * i, 16)].reshape(16 * ROWS, COLS).astype(jnp.float32)
            for h in range(2):
                wide[h, pl.ds(0, 16 * ROWS), :] = part[:, h * LANES : (h + 1) * LANES]
            for r in range(ROWS):
                for h in range(2):
                    flat[pl.ds(16 * i, 16), r * COLS + h * LANES : r * COLS + (h + 1) * LANES] = wide[
                        h, pl.ds(r, 16, stride=ROWS), :
                    ].astype(jnp.bfloat16)
            return carry

        lax.fori_loop(0, rows // 16, flatten, 0)
        if chunk == 0:
            loads[0].wait()
            loads[1].wait()

        def up(n, carry):
            cols = pl.ds(pl.multiple_of(n * 256, 256), 256)
            g = jnp.dot(flat[...], wg[:, cols], preferred_element_type=jnp.float32)
            u = jnp.dot(flat[...], wu[:, cols], preferred_element_type=jnp.float32)
            hid[:, cols] = (g / (1.0 + jnp.exp(-g)) * u).astype(jnp.bfloat16)
            return carry

        lax.fori_loop(0, 3, up, 0)
        if chunk == 0:
            loads[2].wait()

        for r in range(ROWS):
            o = jnp.dot(hid[...], wd[:, r * COLS : (r + 1) * COLS], preferred_element_type=jnp.float32)
            for h in range(2):
                wide[h, pl.ds(r, rows, stride=ROWS), :] = o[:, h * LANES : (h + 1) * LANES]

        def reply(i, carry, first=first):
            j = first + i
            for s in range(CAP):
                for h in range(2):
                    ans[CAP * j + s, :, h * LANES : (h + 1) * LANES] = wide[
                        h, pl.ds(pl.multiple_of((CAP * i + s) * ROWS, ROWS), ROWS), :
                    ].astype(jnp.bfloat16)
            return carry

        def send_back(i, carry, first=first):
            j = first + i
            reply(i, carry)
            pltpu.make_async_remote_copy(
                src_ref=ans.at[pl.ds(CAP * j, CAP)],
                dst_ref=ret.at[pl.ds(CAP * j, CAP)],
                send_sem=ans_sem,
                recv_sem=ret_sem,
                device_id=shifted(ctx, ep, j, -1),
                device_id_type=MESH,
            ).start()
            return carry

        if chunk == 0:
            for s in range(CAP):
                for h in range(2):
                    ret[s, :, h * LANES : (h + 1) * LANES] = wide[h, pl.ds(s * ROWS, ROWS), :].astype(jnp.bfloat16)
        lax.fori_loop(begin - first, half, send_back, 0)

    others = ret.at[pl.ds(CAP, CAP * (N_DEV - 1))]
    pltpu.make_async_copy(others, others, ret_sem).wait()

    def combine(t, carry):
        total = jnp.zeros((ROWS, COLS), jnp.float32)
        for k in range(TOP):
            total += gate_ref[t * TOP + k] * ret[place_ref[t * TOP + k]].astype(jnp.float32)
        for h in range(2):
            wide[h, pl.ds(pl.multiple_of(t * ROWS, ROWS), ROWS), :] = total[:, h * LANES : (h + 1) * LANES]
        return carry

    lax.fori_loop(0, 32, combine, 0)
    for r in range(ROWS):
        for h in range(2):
            out_ref[:, r * COLS + h * LANES : r * COLS + (h + 1) * LANES] = wide[
                h, pl.ds(r, 32, stride=ROWS), :
            ].astype(jnp.bfloat16)

    sent = send.at[pl.ds(CAP, CAP * (N_DEV - 1))]
    pltpu.make_async_copy(sent, sent, send_sem).wait()
    answered = ans.at[pl.ds(CAP, CAP * (N_DEV - 1))]
    pltpu.make_async_copy(answered, answered, ans_sem).wait()


def experts(tokens, places, gates, blocks, w_gate, w_up, w_down):
    smem = pl.BlockSpec(memory_space=pltpu.SMEM)
    vmem = pl.BlockSpec(memory_space=pltpu.VMEM)
    hbm = pl.BlockSpec(memory_space=pl.ANY)
    slots = N_DEV * CAP
    hidden = w_gate.shape[2]
    box = pltpu.VMEM((slots, ROWS, COLS), jnp.bfloat16)
    return pl.pallas_call(
        experts_kernel,
        out_shape=jax.ShapeDtypeStruct((32, D), jnp.bfloat16),
        in_specs=[smem, smem, smem, vmem, hbm, hbm, hbm],
        out_specs=vmem,
        scratch_shapes=[
            pltpu.VMEM((D, hidden), jnp.bfloat16),
            pltpu.VMEM((D, hidden), jnp.bfloat16),
            pltpu.VMEM((hidden, D), jnp.bfloat16),
            box, box, box, box,
            pltpu.VMEM((2, slots // 2 * ROWS, LANES), jnp.float32),
            pltpu.VMEM((slots // 2, D), jnp.bfloat16),
            pltpu.VMEM((slots // 2, hidden), jnp.bfloat16),
            pltpu.SemaphoreType.DMA((3,)),
            pltpu.SemaphoreType.DMA,
            pltpu.SemaphoreType.DMA((2,)),
            pltpu.SemaphoreType.DMA,
            pltpu.SemaphoreType.DMA,
        ],
        compiler_params=pltpu.CompilerParams(
            collective_id=1, has_side_effects=True, vmem_limit_bytes=56 * 1024 * 1024
        ),
        name="experts",
    )(tokens, places, gates, blocks, w_gate, w_up, w_down)


def local(
    stream, queries, keys, values, out_weight, norm_gain, routes, gates, w_gate, w_up, w_down
):
    n_ep = lax.axis_size("ep")
    ctx_index = lax.axis_index("ctx")
    ep_index = lax.axis_index("ep")

    flat_routes = routes.reshape(-1)
    entries = flat_routes.shape[0]
    order = jnp.arange(entries, dtype=jnp.int32)
    same = (flat_routes[:, None] == flat_routes[None, :]) & (order[None, :] < order[:, None])
    rank = jnp.sum(same.astype(jnp.int32), axis=1)
    slot = flat_routes * CAP + rank
    table = jnp.arange(N_DEV * CAP, dtype=jnp.int32)
    tokens = jnp.sum(jnp.where(slot[None, :] == table[:, None], (order // TOP)[None, :], 0), axis=1)
    places = offset_of(ctx_index, ep_index, flat_routes // n_ep, flat_routes % n_ep) * CAP + rank

    resid, blocks = attend(queries, keys, values, stream, norm_gain, out_weight)
    expert_sum = experts(
        tokens, places, gates.reshape(-1), blocks, w_gate, w_up, w_down
    )
    return (resid, expert_sum)


def solution(mesh):
    placed = (
        P("ctx", "ep"),
        P("ctx", "ep"),
        P("ctx", None),
        P("ctx", None),
        P("ep", None),
        P(),
        P(("ctx", "ep"), None),
        P(("ctx", "ep"), None),
        P(("ctx", "ep"), None, None),
        P(("ctx", "ep"), None, None),
        P(("ctx", "ep"), None, None),
    )
    return jax.shard_map(
        local,
        mesh=mesh,
        in_specs=placed,
        out_specs=(P(("ctx", "ep"), None), P(("ctx", "ep"), None)),
        check_vma=False,
    )
```

```python
import functools

import jax
import jax.numpy as jnp
from jax import lax
from jax.experimental import pallas as pl
from jax.experimental.pallas import tpu as pltpu
from jax.sharding import PartitionSpec as P

D = 4096
HD = 128
TOP = 8
CAP = 3
ROWS = 16
COLS = D // ROWS
LANES = 128
MESH = pl.DeviceIdType.MESH
N_DEV = 128


def shifted(ctx, ep, j, sign):
    a, b, c = j % 4, (j // 4) % 4, (j // 16) % 4
    core = (ctx + j // 64) % 2
    z = (ctx // 2 + 4 + sign * ((a + b) % 4)) % 4
    y = ((ep % 2) * 2 + ctx // 8 + 4 + sign * ((a + 2 * b + c) % 4)) % 4
    x = (ep // 2 + 4 + sign * a) % 4
    return (y % 2) * 8 + z * 2 + core, x * 2 + y // 2


def offset_of(ctx, ep, to):
    core = (to >> 3) + ctx & 1
    z = (to >> 4) + 4 - ctx // 2 % 4 & 3
    y = ((to & 1) << 1) + (to >> 6) + 4 - (ep % 2 * 2 + ctx // 8) & 3
    a = (to >> 1 & 3) + 4 - ep // 2 & 3
    b = z + 4 - a & 3
    c = y + 12 - a - 2 * b & 3
    return core * 64 + c * 16 + b * 4 + a


def kv_peer(ctx, ep, o, sign):
    core = ctx % 2
    y = (ep % 2) * 2 + ctx // 8
    z = (ctx // 2 + 4 + sign * (o % 4)) % 4
    step = (o // 4) * (1 + 2 * core)
    y = (y + 4 + sign * step) % 4
    return (y % 2) * 8 + z * 2 + core, (ep // 2) * 2 + y // 2


def ep_peer(ep, o, sign):
    return ((ep // 2 + 4 + sign * (o // 2)) % 4) * 2 + (ep + o) % 2


def layer_kernel(
    q_hbm, k_hbm, v_hbm, stream_hbm, gain_hbm, ow_hbm, routes_hbm, gates_hbm, wg_hbm, wu_hbm, wd_hbm,
    resid_ref, out_ref,
    q_ref, stream_ref, gain_ref, ow, routes_ref, token_ref, place_ref, token_s, place_s, gate_s,
    kall, vall, score, qs, attn, part_out, part_in, stream_in,
    wg, wu, wd, blocks, send, recv, ans, ret, wide, flat, hid,
    in_sem, k_send, v_send, k_recv, v_recv, k_sib, v_sib, st_send, st_recv, p_send, p_recv,
    send_sem, recv_sem, ans_sem, ret_sem,
):
    ctx = lax.axis_index("ctx")
    ep = lax.axis_index("ep")
    rows = q_ref.shape[0]

    def block(c):
        return pl.ds(pl.multiple_of(c * rows, rows), rows)

    head = pl.ds(pl.multiple_of(ep // 2 * HD, HD), HD)
    pairs = (
        (k_hbm.at[:, head], kall.at[block(ctx)]),
        (v_hbm.at[:, head], vall.at[block(ctx)]),
        (routes_hbm, routes_ref),
        (gates_hbm, gate_s),
        (stream_hbm, stream_ref),
        (q_hbm, q_ref),
        (gain_hbm, gain_ref),
        (ow_hbm, ow),
        (wg_hbm.at[0], wg),
        (wu_hbm.at[0], wu),
        (wd_hbm.at[0], wd),
        (token_ref, token_s),
        (place_ref, place_s),
    )
    loads = [pltpu.make_async_copy(s, d, in_sem.at[i]) for i, (s, d) in enumerate(pairs)]
    for load in loads[:11]:
        load.start()
    sibling = (ctx // 2 * 2 + (ctx + 1) % 2, ep)
    barrier = pltpu.get_barrier_semaphore()
    for o in range(1, 8):
        pl.semaphore_signal(barrier, inc=1, device_id=kv_peer(ctx, ep, o, -1), device_id_type=MESH)
        pl.semaphore_signal(barrier, inc=1, device_id=(ctx, ep_peer(ep, o, -1)), device_id_type=MESH)
    pl.semaphore_signal(barrier, inc=1, device_id=sibling, device_id_type=MESH)

    loads[2].wait()
    shape = (N_DEV, 32)
    expert = lax.broadcasted_iota(jnp.int32, shape, 0)
    position = lax.broadcasted_iota(jnp.int32, shape, 1)
    named = [expert == routes_ref[k : k + 1, :] for k in range(TOP)]
    present = named[0]
    for k in range(1, TOP):
        present = present | named[k]
    left = jnp.where(present, position, 32)
    picks = []
    for s in range(CAP):
        picks.append(jnp.min(left, axis=1, keepdims=True))
        left = jnp.where(left > picks[s], left, 32)
    column = lax.broadcasted_iota(jnp.int32, (N_DEV, LANES), 1)
    table = jnp.where(column == 0, picks[0], jnp.where(column == 1, picks[1], picks[2]))
    token_ref[...] = jnp.where(table < 32, table, 0)
    rank = jnp.where(position > picks[0], 1, 0) + jnp.where(position > picks[1], 1, 0)
    slot = offset_of(ctx, ep, expert) * CAP + rank
    for k in range(TOP):
        place_ref[k : k + 1, 0:32] = jnp.sum(jnp.where(named[k], slot, 0), axis=0, keepdims=True)
    loads[11].start()
    loads[12].start()

    loads[0].wait()
    loads[1].wait()
    pl.semaphore_wait(barrier, 15)

    def share(ref, c, send, recv, to):
        return pltpu.make_async_remote_copy(
            src_ref=ref.at[block(c)],
            dst_ref=ref.at[block(c)],
            send_sem=send,
            recv_sem=recv,
            device_id=to,
            device_id_type=MESH,
        )

    for o in (4, 1, 3, 5, 7, 2, 6):
        to = kv_peer(ctx, ep, o, 1)
        share(kall, ctx, k_send, k_recv.at[o], to).start()
        share(vall, ctx, v_send, v_recv.at[o], to).start()
    share(kall, ctx, k_send, k_sib.at[0], sibling).start()
    share(vall, ctx, v_send, v_sib.at[0], sibling).start()
    loads[4].wait()
    for o in range(1, 8):
        to = ep_peer(ep, o, 1)
        pltpu.make_async_remote_copy(
            src_ref=stream_ref.at[pl.ds(pl.multiple_of(to * 32, 32), 32)],
            dst_ref=stream_in.at[o],
            send_sem=st_send,
            recv_sem=st_recv,
            device_id=(ctx, to),
            device_id_type=MESH,
        ).start()

    def landed(ref, c, sem):
        part = ref.at[block(c)]
        pltpu.make_async_copy(part, part, sem).wait()

    for o in (4, 1, 3, 5, 7, 2, 6):
        c = kv_peer(ctx, ep, o, -1)[0]
        landed(kall, c, k_recv.at[o])
        share(kall, c, k_send, k_sib.at[o], sibling).start()
        landed(vall, c, v_recv.at[o])
        share(vall, c, v_send, v_sib.at[o], sibling).start()
    for load in loads[5:8]:
        load.wait()
    for o in range(8):
        c = kv_peer(ctx, ep, o, -1)[0]
        other = c // 2 * 2 + (c + 1) % 2
        landed(kall, other, k_sib.at[o])
        landed(vall, other, v_sib.at[o])

    width = score.shape[2]
    factor = HD ** (-0.5) * 1.4426950408889634
    heads = q_ref.shape[1] // HD

    def give(o, n):
        cols = pl.ds(n * (D // 4), D // 4)
        pltpu.make_async_remote_copy(
            src_ref=part_out.at[o, :, cols],
            dst_ref=part_in.at[o, :, cols],
            send_sem=p_send,
            recv_sem=p_recv,
            device_id=(ctx, ep_peer(ep, o, 1)),
            device_id_type=MESH,
        ).start()

    def one_part(i, carry):
        dx = (2 + 3 * i) % 4
        x = (ep // 2 + dx) % 4
        first = pl.multiple_of(x * 64, 64)
        for h in range(heads):
            qs[64 * h : 64 * h + 64, :] = q_ref[pl.ds(first, 64), HD * h : HD * h + HD]
        last = (ctx * rows + first) // width

        def scores(t):
            keys = kall[pl.ds(pl.multiple_of(t * width, width), width), :]
            return lax.dot_general(
                qs[...], keys, (((1,), (1,)), ((), ())), preferred_element_type=jnp.float32
            )

        def top_of(s, top):
            for j in range(width // LANES):
                top = jnp.maximum(top, s[:, j * LANES : (j + 1) * LANES])
            return top

        def look(t, top):
            s = scores(t)
            score[t] = s
            return top_of(s, top)

        top = lax.fori_loop(0, last, look, jnp.full((64 * heads, LANES), -1e30, jnp.float32))
        s = scores(last)
        query_pos = ctx * rows + first + lax.broadcasted_iota(jnp.int32, s.shape, 0) % 64
        key_pos = last * width + lax.broadcasted_iota(jnp.int32, s.shape, 1)
        s = jnp.where(key_pos <= query_pos, s, -1e30)
        score[last] = s
        top = jnp.max(top_of(s, top), axis=1, keepdims=True)

        def mix(t, state):
            total, mixed = state
            weight = jnp.exp2((score[t] - top) * factor)
            for j in range(width // LANES):
                total = total + weight[:, j * LANES : (j + 1) * LANES]
            mixed = mixed + jnp.dot(
                weight.astype(jnp.bfloat16),
                vall[pl.ds(pl.multiple_of(t * width, width), width), :],
                preferred_element_type=jnp.float32,
            )
            return total, mixed

        zero = jnp.zeros((64 * heads, LANES), jnp.float32)
        total, mixed = lax.fori_loop(0, last + 1, mix, (zero, zero))
        mixed = (mixed / jnp.sum(total, axis=1, keepdims=True)).astype(jnp.bfloat16)
        for h in range(heads):
            attn[:, HD * h : HD * h + HD] = mixed[64 * h : 64 * h + 64, :]

        def project(n, carry):
            cols = pl.ds(pl.multiple_of(n * 512, 512), 512)
            p = jnp.dot(attn[...], ow[:, cols], preferred_element_type=jnp.float32).astype(jnp.bfloat16)
            for y_hi in range(2):
                part_out[2 * dx + (ep + y_hi) % 2, :, cols] = p[32 * y_hi : 32 * y_hi + 32, :]
            return carry

        lax.fori_loop(0, D // 512, project, 0)

        @pl.when(i == 0)
        def _():
            for n in range(4):
                give(5, n)
                give(4, n)

        @pl.when(i == 2)
        def _():
            for n in range(4):
                give(1, n)

        return carry

    lax.fori_loop(0, 4, one_part, 0)
    for n in range(4):
        for o in (2, 6, 3, 7):
            give(o, n)

    def all_of(ref, sem):
        part = ref.at[pl.ds(1, 7)]
        pltpu.make_async_copy(part, part, sem).wait()

    all_of(stream_in, st_recv)
    all_of(part_in, p_recv)
    squares = jnp.zeros((32, LANES), jnp.float32)
    for o in range(8):
        source = ep_peer(ep, o, -1)
        cols = pl.ds(pl.multiple_of(source * 512, 512), 512)
        if o == 0:
            own = stream_ref[pl.ds(pl.multiple_of(ep * 32, 32), 32), :]
        else:
            own = stream_in[o]
        total = part_out[0, :, cols].astype(jnp.float32)
        for p in range(1, 8):
            total += part_in[p, :, cols].astype(jnp.float32)
        total = (total + own.astype(jnp.float32)).astype(jnp.bfloat16)
        resid_ref[:, cols] = total
        total = total.astype(jnp.float32)
        for j in range(4):
            piece = total[:, j * LANES : (j + 1) * LANES]
            squares += piece * piece
    inverse = lax.rsqrt(jnp.sum(squares, axis=1, keepdims=True) / D + 1e-06)
    for r in range(ROWS):
        for h in range(2):
            at = r * COLS + h * LANES
            wide[h, pl.ds(r, 32, stride=ROWS), :] = (
                resid_ref[:, at : at + LANES].astype(jnp.float32) * inverse * gain_ref[:, at : at + LANES]
            )

    def store(t, carry):
        for h in range(2):
            blocks[t, :, h * LANES : (h + 1) * LANES] = wide[
                h, pl.ds(pl.multiple_of(t * ROWS, ROWS), ROWS), :
            ].astype(jnp.bfloat16)
        return carry

    lax.fori_loop(0, 32, store, 0)
    for i in (3, 11, 12):
        loads[i].wait()

    def pack(into, j, to_ctx, to_ep):
        to = to_ctx * 8 + to_ep
        for s in range(CAP):
            into[CAP * j + s] = blocks[token_s[to, s]]

    def dispatch(j, carry):
        to = shifted(ctx, ep, j, 1)
        pack(send, j, *to)
        pltpu.make_async_remote_copy(
            src_ref=send.at[pl.ds(CAP * j, CAP)],
            dst_ref=recv.at[pl.ds(CAP * j, CAP)],
            send_sem=send_sem,
            recv_sem=recv_sem.at[j // 64],
            device_id=to,
            device_id_type=MESH,
        ).start()
        return carry

    lax.fori_loop(1, N_DEV, dispatch, 0)
    pack(recv, 0, ctx, ep)

    half = N_DEV // 2
    count = half * CAP
    for chunk in range(2):
        first = chunk * half
        begin = max(first, 1)
        arrived = recv.at[pl.ds(CAP * begin, CAP * (first + half - begin))]
        pltpu.make_async_copy(arrived, arrived, recv_sem.at[chunk]).wait()

        def flatten(i, carry, first=first):
            part = recv[pl.ds(CAP * first + 16 * i, 16)].reshape(16 * ROWS, COLS).astype(jnp.float32)
            for h in range(2):
                wide[h, pl.ds(0, 16 * ROWS), :] = part[:, h * LANES : (h + 1) * LANES]
            for r in range(ROWS):
                for h in range(2):
                    flat[pl.ds(16 * i, 16), r * COLS + h * LANES : r * COLS + (h + 1) * LANES] = wide[
                        h, pl.ds(r, 16, stride=ROWS), :
                    ].astype(jnp.bfloat16)
            return carry

        lax.fori_loop(0, count // 16, flatten, 0)
        if chunk == 0:
            loads[8].wait()
            loads[9].wait()

        def up(n, carry):
            cols = pl.ds(pl.multiple_of(n * 256, 256), 256)
            g = jnp.dot(flat[...], wg[:, cols], preferred_element_type=jnp.float32)
            u = jnp.dot(flat[...], wu[:, cols], preferred_element_type=jnp.float32)
            hid[:, cols] = (g / (1.0 + jnp.exp(-g)) * u).astype(jnp.bfloat16)
            return carry

        lax.fori_loop(0, 3, up, 0)
        if chunk == 0:
            loads[10].wait()

        for r in range(ROWS):
            o = jnp.dot(hid[...], wd[:, r * COLS : (r + 1) * COLS], preferred_element_type=jnp.float32)
            for h in range(2):
                wide[h, pl.ds(r, count, stride=ROWS), :] = o[:, h * LANES : (h + 1) * LANES]

        def reply(i, carry, first=first):
            j = first + i
            for s in range(CAP):
                for h in range(2):
                    ans[CAP * j + s, :, h * LANES : (h + 1) * LANES] = wide[
                        h, pl.ds(pl.multiple_of((CAP * i + s) * ROWS, ROWS), ROWS), :
                    ].astype(jnp.bfloat16)
            return carry

        def send_back(i, carry, first=first):
            j = first + i
            reply(i, carry)
            pltpu.make_async_remote_copy(
                src_ref=ans.at[pl.ds(CAP * j, CAP)],
                dst_ref=ret.at[pl.ds(CAP * j, CAP)],
                send_sem=ans_sem,
                recv_sem=ret_sem,
                device_id=shifted(ctx, ep, j, -1),
                device_id_type=MESH,
            ).start()
            return carry

        if chunk == 0:
            for s in range(CAP):
                for h in range(2):
                    ret[s, :, h * LANES : (h + 1) * LANES] = wide[h, pl.ds(s * ROWS, ROWS), :].astype(jnp.bfloat16)
        lax.fori_loop(begin - first, half, send_back, 0)

    others = ret.at[pl.ds(CAP, CAP * (N_DEV - 1))]
    pltpu.make_async_copy(others, others, ret_sem).wait()

    def combine(t, carry):
        total = jnp.zeros((ROWS, COLS), jnp.float32)
        for k in range(TOP):
            total += gate_s[k, t] * ret[place_s[k, t]].astype(jnp.float32)
        for h in range(2):
            wide[h, pl.ds(pl.multiple_of(t * ROWS, ROWS), ROWS), :] = total[:, h * LANES : (h + 1) * LANES]
        return carry

    lax.fori_loop(0, 32, combine, 0)
    for r in range(ROWS):
        for h in range(2):
            out_ref[:, r * COLS + h * LANES : r * COLS + (h + 1) * LANES] = wide[
                h, pl.ds(r, 32, stride=ROWS), :
            ].astype(jnp.bfloat16)

    sent = send.at[pl.ds(CAP, CAP * (N_DEV - 1))]
    pltpu.make_async_copy(sent, sent, send_sem).wait()
    answered = ans.at[pl.ds(CAP, CAP * (N_DEV - 1))]
    pltpu.make_async_copy(answered, answered, ans_sem).wait()

    for ref, sem in ((kall, k_send), (vall, v_send)):
        gone = ref.at[pl.ds(0, 15 * rows)]
        pltpu.make_async_copy(gone, gone, sem).wait()
    all_of(stream_in, st_send)
    all_of(part_out, p_send)


def local(
    stream, queries, keys, values, out_weight, norm_gain, routes, gates, w_gate, w_up, w_down
):
    rows, width = queries.shape
    positions = rows * 16
    slots = N_DEV * CAP
    hidden = w_gate.shape[2]
    bf16, f32, i32 = jnp.bfloat16, jnp.float32, jnp.int32
    hbm = pl.BlockSpec(memory_space=pl.ANY)
    vmem = pl.BlockSpec(memory_space=pltpu.VMEM)
    one = pltpu.SemaphoreType.DMA
    two = pltpu.SemaphoreType.DMA((2,))
    eight = pltpu.SemaphoreType.DMA((8,))
    box = pltpu.VMEM((slots, ROWS, COLS), bf16)
    return pl.pallas_call(
        layer_kernel,
        out_shape=(jax.ShapeDtypeStruct((32, D), bf16), jax.ShapeDtypeStruct((32, D), bf16)),
        in_specs=[hbm] * 11,
        out_specs=(vmem, vmem),
        scratch_shapes=[
            pltpu.VMEM(queries.shape, bf16),
            pltpu.VMEM(stream.shape, bf16),
            pltpu.VMEM((1, D), f32),
            pltpu.VMEM(out_weight.shape, bf16),
            pltpu.VMEM((TOP, 32), i32),
            pltpu.VMEM((N_DEV, LANES), i32),
            pltpu.VMEM((TOP, LANES), i32),
            pltpu.SMEM((N_DEV, LANES), i32),
            pltpu.SMEM((TOP, LANES), i32),
            pltpu.SMEM((TOP, 32), f32),
            pltpu.VMEM((positions, HD), bf16),
            pltpu.VMEM((positions, HD), bf16),
            pltpu.VMEM((positions // 1024, width // HD * 64, 1024), f32),
            pltpu.VMEM((width // HD * 64, HD), bf16),
            pltpu.VMEM((64, width), bf16),
            pltpu.VMEM((8, 32, D), bf16),
            pltpu.VMEM((8, 32, D), bf16),
            pltpu.VMEM((8, 32, D // 8), bf16),
            pltpu.VMEM((D, hidden), bf16),
            pltpu.VMEM((D, hidden), bf16),
            pltpu.VMEM((hidden, D), bf16),
            pltpu.VMEM((32, ROWS, COLS), bf16),
            box, box, box, box,
            pltpu.VMEM((2, slots // 2 * ROWS, LANES), f32),
            pltpu.VMEM((slots // 2, D), bf16),
            pltpu.VMEM((slots // 2, hidden), bf16),
            pltpu.SemaphoreType.DMA((13,)),
            one, one, eight, eight, eight, eight, one, one, one, one,
            one, two, one, one,
        ],
        compiler_params=pltpu.CompilerParams(
            collective_id=0, has_side_effects=True, vmem_limit_bytes=60 * 1024 * 1024
        ),
        name="layer",
    )(
        queries, keys, values, stream, norm_gain.reshape(1, D), out_weight, routes.T, gates.T,
        w_gate, w_up, w_down,
    )


def solution(mesh):
    placed = (
        P("ctx", "ep"),
        P("ctx", "ep"),
        P("ctx", None),
        P("ctx", None),
        P("ep", None),
        P(),
        P(("ctx", "ep"), None),
        P(("ctx", "ep"), None),
        P(("ctx", "ep"), None, None),
        P(("ctx", "ep"), None, None),
        P(("ctx", "ep"), None, None),
    )
    return jax.shard_map(
        local,
        mesh=mesh,
        in_specs=placed,
        out_specs=(P(("ctx", "ep"), None), P(("ctx", "ep"), None)),
        check_vma=False,
    )
```

```python
import functools

import jax
import jax.numpy as jnp
from jax import lax
from jax.experimental import pallas as pl
from jax.experimental.pallas import tpu as pltpu
from jax.sharding import PartitionSpec as P

D = 4096
HD = 128
TOP = 8
CAP = 3
ROWS = 16
COLS = D // ROWS
LANES = 128
MESH = pl.DeviceIdType.MESH
N_DEV = 128


def shifted(ctx, ep, j, sign):
    a, b, c = j % 4, (j // 4) % 4, (j // 16) % 4
    core = (ctx + j // 64) % 2
    z = (ctx // 2 + 4 + sign * ((a + b) % 4)) % 4
    y = ((ep % 2) * 2 + ctx // 8 + 4 + sign * ((a + 2 * b + c) % 4)) % 4
    x = (ep // 2 + 4 + sign * a) % 4
    return (y % 2) * 8 + z * 2 + core, x * 2 + y // 2


def offset_of(ctx, ep, to):
    core = (to >> 3) + ctx & 1
    z = (to >> 4) + 4 - ctx // 2 % 4 & 3
    y = ((to & 1) << 1) + (to >> 6) + 4 - (ep % 2 * 2 + ctx // 8) & 3
    a = (to >> 1 & 3) + 4 - ep // 2 & 3
    b = z + 4 - a & 3
    c = y + 12 - a - 2 * b & 3
    return core * 64 + c * 16 + b * 4 + a


def kv_peer(ctx, ep, o, sign):
    core = ctx % 2
    y = (ep % 2) * 2 + ctx // 8
    z = (ctx // 2 + 4 + sign * (o % 4)) % 4
    step = (o // 4) * (1 + 2 * core)
    y = (y + 4 + sign * step) % 4
    return (y % 2) * 8 + z * 2 + core, (ep // 2) * 2 + y // 2


def ep_peer(ep, o, sign):
    return ((ep // 2 + 4 + sign * (o // 2)) % 4) * 2 + (ep + o) % 2


def layer_kernel(
    q_hbm, k_hbm, v_hbm, stream_hbm, gain_hbm, ow_hbm, routes_hbm, gates_hbm, wg_hbm, wu_hbm, wd_hbm,
    resid_ref, out_ref,
    q_ref, stream_ref, gain_ref, ow, routes_ref, token_ref, place_ref, token_s, place_s, gate_s,
    kall, vall, score, qs, attn, part_out, along_in, flip_in, both_out, both_in, last_out, last_in, stream_in,
    wg, wu, wd, blocks, send, recv, ans, ret, wide, flat, hid,
    in_sem, k_send, v_send, k_recv, v_recv, k_sib, v_sib, st_send, st_recv,
    along_send, along_recv, flip_send, flip_recv, both_send, both_recv, last_send, last_recv,
    send_sem, recv_sem, ans_sem, ret_sem,
):
    ctx = lax.axis_index("ctx")
    ep = lax.axis_index("ep")
    rows = q_ref.shape[0]

    def block(c):
        return pl.ds(pl.multiple_of(c * rows, rows), rows)

    head = pl.ds(pl.multiple_of(ep // 2 * HD, HD), HD)
    pairs = (
        (k_hbm.at[:, head], kall.at[block(ctx)]),
        (v_hbm.at[:, head], vall.at[block(ctx)]),
        (routes_hbm, routes_ref),
        (gates_hbm, gate_s),
        (stream_hbm, stream_ref),
        (q_hbm, q_ref),
        (gain_hbm, gain_ref),
        (ow_hbm, ow),
        (wg_hbm.at[0], wg),
        (wu_hbm.at[0], wu),
        (wd_hbm.at[0], wd),
        (token_ref, token_s),
        (place_ref, place_s),
    )
    loads = [pltpu.make_async_copy(s, d, in_sem.at[i]) for i, (s, d) in enumerate(pairs)]
    for load in loads[:11]:
        load.start()
    sibling = (ctx // 2 * 2 + (ctx + 1) % 2, ep)
    barrier = pltpu.get_barrier_semaphore()
    for o in range(1, 5):
        pl.semaphore_signal(barrier, inc=1, device_id=kv_peer(ctx, ep, o, -1), device_id_type=MESH)
    for o in range(1, 8):
        pl.semaphore_signal(barrier, inc=1, device_id=(ctx, ep_peer(ep, o, -1)), device_id_type=MESH)
    pl.semaphore_signal(barrier, inc=1, device_id=sibling, device_id_type=MESH)

    loads[0].wait()
    loads[1].wait()
    pl.semaphore_wait(barrier, 12)

    def share(ref, c, send, recv, to):
        return pltpu.make_async_remote_copy(
            src_ref=ref.at[block(c)],
            dst_ref=ref.at[block(c)],
            send_sem=send,
            recv_sem=recv,
            device_id=to,
            device_id_type=MESH,
        )

    for o in (4, 1, 3, 2):
        to = kv_peer(ctx, ep, o, 1)
        share(kall, ctx, k_send, k_recv.at[o], to).start()
        share(vall, ctx, v_send, v_recv.at[o], to).start()
    share(kall, ctx, k_send, k_sib.at[0], sibling).start()
    share(vall, ctx, v_send, v_sib.at[0], sibling).start()
    loads[4].wait()
    stream_in[0] = stream_ref[pl.ds(pl.multiple_of(ep * 32, 32), 32), :]
    for o in range(1, 8):
        to = ep_peer(ep, o, 1)
        pltpu.make_async_remote_copy(
            src_ref=stream_ref.at[pl.ds(pl.multiple_of(to * 32, 32), 32)],
            dst_ref=stream_in.at[o],
            send_sem=st_send,
            recv_sem=st_recv,
            device_id=(ctx, to),
            device_id_type=MESH,
        ).start()

    def landed(ref, c, sem):
        part = ref.at[block(c)]
        pltpu.make_async_copy(part, part, sem).wait()

    loads[2].wait()
    shape = (N_DEV, 32)
    expert = lax.broadcasted_iota(jnp.int32, shape, 0)
    position = lax.broadcasted_iota(jnp.int32, shape, 1)
    named = [expert == routes_ref[k : k + 1, :] for k in range(TOP)]
    present = named[0]
    for k in range(1, TOP):
        present = present | named[k]
    left = jnp.where(present, position, 32)
    picks = []
    for s in range(CAP):
        picks.append(jnp.min(left, axis=1, keepdims=True))
        left = jnp.where(left > picks[s], left, 32)
    column = lax.broadcasted_iota(jnp.int32, (N_DEV, LANES), 1)
    table = jnp.where(column == 0, picks[0], jnp.where(column == 1, picks[1], picks[2]))
    token_ref[...] = jnp.where(table < 32, table, 0)
    rank = jnp.where(position > picks[0], 1, 0) + jnp.where(position > picks[1], 1, 0)
    slot = offset_of(ctx, ep, expert) * CAP + rank
    for k in range(TOP):
        place_ref[k : k + 1, 0:32] = jnp.sum(jnp.where(named[k], slot, 0), axis=0, keepdims=True)
    loads[11].start()
    loads[12].start()

    across = kv_peer(ctx, ep, 4, 1)
    for o in (1, 3, 4, 2, 5, 7, 6):
        c = kv_peer(ctx, ep, o, -1)[0]
        for ref, out_sem, at_sem, sib in ((kall, k_send, k_recv, k_sib), (vall, v_send, v_recv, v_sib)):
            landed(ref, c, at_sem.at[o])
            if o < 4:
                share(ref, c, out_sem, at_sem.at[o + 4], across).start()
            share(ref, c, out_sem, sib.at[o], sibling).start()
    for load in loads[5:8]:
        load.wait()
    for o in range(8):
        c = kv_peer(ctx, ep, o, -1)[0]
        other = c // 2 * 2 + (c + 1) % 2
        landed(kall, other, k_sib.at[o])
        landed(vall, other, v_sib.at[o])

    width = score.shape[2]
    factor = HD ** (-0.5) * 1.4426950408889634
    heads = q_ref.shape[1] // HD

    half_d = D // 2
    late = pl.ds(half_d, half_d)
    own_rows = pl.ds(pl.multiple_of(ep % 2 * 32, 32), 32)
    other_rows = pl.ds(pl.multiple_of((ep + 1) % 2 * 32, 32), 32)
    partner = ep_peer(ep, 1, 1)

    def landed_flip(dx):
        part = flip_in.at[dx]
        pltpu.make_async_copy(part, part, flip_recv.at[dx]).wait()

    def one_part(i, state):
        code, before = state
        dx = code % 4
        first = pl.multiple_of((ep // 2 + dx) % 4 * 64, 64)
        for h in range(heads):
            qs[64 * h : 64 * h + 64, :] = q_ref[pl.ds(first, 64), HD * h : HD * h + HD]
        last = (ctx * rows + first) // width
        lowest = jnp.full((64 * heads, LANES), -1e30, jnp.float32)
        zero = jnp.zeros((64 * heads, LANES), jnp.float32)

        def scores(t):
            keys = kall[pl.ds(pl.multiple_of(t * width, width), width), :]
            return lax.dot_general(
                qs[...], keys, (((1,), (1,)), ((), ())), preferred_element_type=jnp.float32
            )

        def look(t, top, masked=False):
            s = scores(t)
            if masked:
                query_pos = ctx * rows + first + lax.broadcasted_iota(jnp.int32, s.shape, 0) % 64
                key_pos = t * width + lax.broadcasted_iota(jnp.int32, s.shape, 1)
                s = jnp.where(key_pos <= query_pos, s, -1e30)
            score[t] = s
            for j in range(width // LANES):
                top = jnp.maximum(top, s[:, j * LANES : (j + 1) * LANES])
            return top

        def mix(t, state, top):
            total, mixed = state
            weight = jnp.exp2((score[t] - top) * factor)
            for j in range(width // LANES):
                total = total + weight[:, j * LANES : (j + 1) * LANES]
            mixed = mixed + jnp.dot(
                weight.astype(jnp.bfloat16),
                vall[pl.ds(pl.multiple_of(t * width, width), width), :],
                preferred_element_type=jnp.float32,
            )
            return total, mixed

        def finish(total, mixed):
            mixed = (mixed / jnp.sum(total, axis=1, keepdims=True)).astype(jnp.bfloat16)
            for h in range(heads):
                attn[:, HD * h : HD * h + HD] = mixed[64 * h : 64 * h + 64, :]

        tiles = score.shape[0]

        @pl.when(last == tiles - 1)
        def _():
            top = lowest
            for t in range(tiles):
                top = look(t, top, t == tiles - 1)
            top = jnp.max(top, axis=1, keepdims=True)
            state = zero, zero
            for t in range(tiles):
                state = mix(t, state, top)
            finish(*state)

        @pl.when(last < tiles - 1)
        def _():
            top = look(last, lax.fori_loop(0, last, look, lowest), True)
            top = jnp.max(top, axis=1, keepdims=True)
            finish(*lax.fori_loop(0, last + 1, functools.partial(mix, top=top), (zero, zero)))

        p = jnp.dot(attn[...], ow[...], preferred_element_type=jnp.float32).astype(jnp.bfloat16)
        part_out[dx] = p

        pltpu.make_async_remote_copy(
            src_ref=part_out.at[dx, other_rows, late],
            dst_ref=flip_in.at[dx],
            send_sem=flip_send,
            recv_sem=flip_recv.at[dx],
            device_id=(ctx, partner),
            device_id_type=MESH,
        ).start()

        @pl.when(dx > 0)
        def _():
            for n in range(2):
                cols = pl.ds(n * (half_d // 2), half_d // 2)
                pltpu.make_async_remote_copy(
                    src_ref=part_out.at[dx, :, cols],
                    dst_ref=along_in.at[dx, :, cols],
                    send_sem=along_send,
                    recv_sem=along_recv,
                    device_id=(ctx, ep_peer(ep, 2 * dx, 1)),
                    device_id_type=MESH,
                ).start()

        @pl.when(i > 0)
        def _():
            landed_flip(before)
            both = part_out[before, own_rows, late].astype(jnp.float32) + flip_in[before].astype(jnp.float32)
            both_out[before] = both.astype(jnp.bfloat16)
            pltpu.make_async_remote_copy(
                src_ref=both_out.at[before],
                dst_ref=both_in.at[before],
                send_sem=both_send,
                recv_sem=both_recv,
                device_id=(ctx, ep_peer(ep, 2 * before, 1)),
                device_id_type=MESH,
            ).start()

        return code // 4, dx

    lax.fori_loop(0, 4, one_part, (2 + 1 * 4 + 3 * 16 + 0 * 64, 0))

    def three_of(ref, sem):
        part = ref.at[pl.ds(1, 3)]
        pltpu.make_async_copy(part, part, sem).wait()

    three_of(along_in, along_recv)
    for n in range(4):
        cols = slice(n * 512, n * 512 + 512)
        total = part_out[0, other_rows, cols].astype(jnp.float32)
        for d in range(1, 4):
            total += along_in[d, other_rows, cols].astype(jnp.float32)
        last_out[:, cols] = total.astype(jnp.bfloat16)
    last = pltpu.make_async_remote_copy(
        src_ref=last_out,
        dst_ref=last_in,
        send_sem=last_send,
        recv_sem=last_recv,
        device_id=(ctx, partner),
        device_id_type=MESH,
    )
    last.start()

    def all_of(ref, sem):
        part = ref.at[pl.ds(1, 7)]
        pltpu.make_async_copy(part, part, sem).wait()

    all_of(stream_in, st_recv)
    landed_flip(0)
    three_of(both_in, both_recv)
    squares = jnp.zeros((32, LANES), jnp.float32)
    for g in (4, 5, 6, 7, 0, 1, 2, 3):
        cols = slice(512 * g, 512 * g + 512)
        if g == 0:
            last.wait_recv()
        total = part_out[0, own_rows, cols].astype(jnp.float32)
        if g < 4:
            total += last_in[:, cols].astype(jnp.float32)
            for d in range(1, 4):
                total += along_in[d, own_rows, cols].astype(jnp.float32)
        else:
            there = slice(512 * g - half_d, 512 * g - half_d + 512)
            total += flip_in[0, :, there].astype(jnp.float32)
            for d in range(1, 4):
                total += both_in[d, :, there].astype(jnp.float32)
        own = stream_in[(ep // 2 + 4 - g // 2) % 4 * 2 + (ep + g) % 2]
        total = (total + own.astype(jnp.float32)).astype(jnp.bfloat16)
        resid_ref[:, cols] = total
        total = total.astype(jnp.float32)
        for j in range(4):
            piece = total[:, j * LANES : (j + 1) * LANES]
            squares += piece * piece
    inverse = lax.rsqrt(jnp.sum(squares, axis=1, keepdims=True) / D + 1e-06)
    for r in range(ROWS):
        for h in range(2):
            at = r * COLS + h * LANES
            wide[h, pl.ds(r, 32, stride=ROWS), :] = (
                resid_ref[:, at : at + LANES].astype(jnp.float32) * inverse * gain_ref[:, at : at + LANES]
            )

    def store(t, carry):
        for h in range(2):
            blocks[t, :, h * LANES : (h + 1) * LANES] = wide[
                h, pl.ds(pl.multiple_of(t * ROWS, ROWS), ROWS), :
            ].astype(jnp.bfloat16)
        return carry

    lax.fori_loop(0, 32, store, 0)
    for i in (3, 11, 12):
        loads[i].wait()

    def pack(into, j, to_ctx, to_ep):
        to = to_ctx * 8 + to_ep
        for s in range(CAP):
            into[CAP * j + s] = blocks[token_s[to, s]]

    def dispatch(j, carry):
        to = shifted(ctx, ep, j, 1)
        pack(send, j, *to)
        pltpu.make_async_remote_copy(
            src_ref=send.at[pl.ds(CAP * j, CAP)],
            dst_ref=recv.at[pl.ds(CAP * j, CAP)],
            send_sem=send_sem,
            recv_sem=recv_sem.at[j // 64],
            device_id=to,
            device_id_type=MESH,
        ).start()
        return carry

    lax.fori_loop(1, N_DEV, dispatch, 0)
    pack(recv, 0, ctx, ep)

    half = N_DEV // 2
    count = half * CAP
    def one_chunk(chunk, carry):
        first = chunk * half

        def wait_for(begin, end, sem):
            arrived = recv.at[pl.ds(CAP * begin, CAP * (end - begin))]
            pltpu.make_async_copy(arrived, arrived, sem).wait()

        @pl.when(chunk == 0)
        def _():
            wait_for(1, half, recv_sem.at[0])

        @pl.when(chunk == 1)
        def _():
            wait_for(half, N_DEV, recv_sem.at[1])

        def flatten(i, carry):
            part = recv[pl.ds(CAP * first + 16 * i, 16)].reshape(16 * ROWS, COLS).astype(jnp.float32)
            for h in range(2):
                wide[h, pl.ds(0, 16 * ROWS), :] = part[:, h * LANES : (h + 1) * LANES]
            for r in range(ROWS):
                for h in range(2):
                    flat[pl.ds(16 * i, 16), r * COLS + h * LANES : r * COLS + (h + 1) * LANES] = wide[
                        h, pl.ds(r, 16, stride=ROWS), :
                    ].astype(jnp.bfloat16)
            return carry

        lax.fori_loop(0, count // 16, flatten, 0)

        @pl.when(chunk == 0)
        def _():
            for load in loads[8:11]:
                load.wait()

        def up(n, carry):
            cols = pl.ds(pl.multiple_of(n * 256, 256), 256)
            g = jnp.dot(flat[...], wg[:, cols], preferred_element_type=jnp.float32)
            u = jnp.dot(flat[...], wu[:, cols], preferred_element_type=jnp.float32)
            hid[:, cols] = (g / (1.0 + jnp.exp(-g)) * u).astype(jnp.bfloat16)
            return carry

        lax.fori_loop(0, 3, up, 0)

        def down(r, carry):
            cols = pl.ds(pl.multiple_of(r * COLS, COLS), COLS)
            o = jnp.dot(hid[...], wd[:, cols], preferred_element_type=jnp.float32)
            for h in range(2):
                wide[h, pl.ds(r, count, stride=ROWS), :] = o[:, h * LANES : (h + 1) * LANES]
            return carry

        lax.fori_loop(0, ROWS, down, 0)

        def reply(into, at, i):
            for s in range(CAP):
                for h in range(2):
                    into[at + s, :, h * LANES : (h + 1) * LANES] = wide[
                        h, pl.ds(pl.multiple_of((CAP * i + s) * ROWS, ROWS), ROWS), :
                    ].astype(jnp.bfloat16)

        def send_back(i, carry):
            j = first + i
            reply(ans, CAP * j, i)
            pltpu.make_async_remote_copy(
                src_ref=ans.at[pl.ds(CAP * j, CAP)],
                dst_ref=ret.at[pl.ds(CAP * j, CAP)],
                send_sem=ans_sem,
                recv_sem=ret_sem,
                device_id=shifted(ctx, ep, j, -1),
                device_id_type=MESH,
            ).start()
            return carry

        @pl.when(chunk == 0)
        def _():
            reply(ret, 0, 0)

        lax.fori_loop(1 - chunk, half, send_back, 0)
        return carry

    lax.fori_loop(0, 2, one_chunk, 0)

    others = ret.at[pl.ds(CAP, CAP * (N_DEV - 1))]
    pltpu.make_async_copy(others, others, ret_sem).wait()

    def combine(t, carry):
        total = jnp.zeros((ROWS, COLS), jnp.float32)
        for k in range(TOP):
            total += gate_s[k, t] * ret[place_s[k, t]].astype(jnp.float32)
        for h in range(2):
            wide[h, pl.ds(pl.multiple_of(t * ROWS, ROWS), ROWS), :] = total[:, h * LANES : (h + 1) * LANES]
        return carry

    lax.fori_loop(0, 32, combine, 0)
    for r in range(ROWS):
        for h in range(2):
            out_ref[:, r * COLS + h * LANES : r * COLS + (h + 1) * LANES] = wide[
                h, pl.ds(r, 32, stride=ROWS), :
            ].astype(jnp.bfloat16)

    sent = send.at[pl.ds(CAP, CAP * (N_DEV - 1))]
    pltpu.make_async_copy(sent, sent, send_sem).wait()
    answered = ans.at[pl.ds(CAP, CAP * (N_DEV - 1))]
    pltpu.make_async_copy(answered, answered, ans_sem).wait()

    for ref, sem in ((kall, k_send), (vall, v_send)):
        gone = ref.at[pl.ds(0, 15 * rows)]
        pltpu.make_async_copy(gone, gone, sem).wait()
    all_of(stream_in, st_send)
    gone = flip_in
    pltpu.make_async_copy(gone, gone, flip_send).wait()
    three_of(along_in, along_send)
    three_of(both_out, both_send)
    last.wait_send()


def local(
    stream, queries, keys, values, out_weight, norm_gain, routes, gates, w_gate, w_up, w_down
):
    rows, width = queries.shape
    positions = rows * 16
    slots = N_DEV * CAP
    hidden = w_gate.shape[2]
    bf16, f32, i32 = jnp.bfloat16, jnp.float32, jnp.int32
    hbm = pl.BlockSpec(memory_space=pltpu.HBM)
    vmem = pl.BlockSpec(memory_space=pltpu.VMEM)
    one = pltpu.SemaphoreType.DMA
    two = pltpu.SemaphoreType.DMA((2,))
    four = pltpu.SemaphoreType.DMA((4,))
    eight = pltpu.SemaphoreType.DMA((8,))
    box = pltpu.VMEM((slots, ROWS, COLS), bf16)
    return pl.pallas_call(
        layer_kernel,
        out_shape=(jax.ShapeDtypeStruct((32, D), bf16), jax.ShapeDtypeStruct((32, D), bf16)),
        in_specs=[hbm] * 11,
        out_specs=(vmem, vmem),
        scratch_shapes=[
            pltpu.VMEM(queries.shape, bf16),
            pltpu.VMEM(stream.shape, bf16),
            pltpu.VMEM((1, D), f32),
            pltpu.VMEM(out_weight.shape, bf16),
            pltpu.VMEM((TOP, 32), i32),
            pltpu.VMEM((N_DEV, LANES), i32),
            pltpu.VMEM((TOP, LANES), i32),
            pltpu.SMEM((N_DEV, LANES), i32),
            pltpu.SMEM((TOP, LANES), i32),
            pltpu.SMEM((TOP, 32), f32),
            pltpu.VMEM((positions, HD), bf16),
            pltpu.VMEM((positions, HD), bf16),
            pltpu.VMEM((positions // 1024, width // HD * 64, 1024), f32),
            pltpu.VMEM((width // HD * 64, HD), bf16),
            pltpu.VMEM((64, width), bf16),
            pltpu.VMEM((4, 64, D), bf16),
            pltpu.VMEM((4, 64, D // 2), bf16),
            pltpu.VMEM((4, 32, D // 2), bf16),
            pltpu.VMEM((4, 32, D // 2), bf16),
            pltpu.VMEM((4, 32, D // 2), bf16),
            pltpu.VMEM((32, D // 2), bf16),
            pltpu.VMEM((32, D // 2), bf16),
            pltpu.VMEM((8, 32, D // 8), bf16),
            pltpu.VMEM((D, hidden), bf16),
            pltpu.VMEM((D, hidden), bf16),
            pltpu.VMEM((hidden, D), bf16),
            pltpu.VMEM((32, ROWS, COLS), bf16),
            box, box, box, box,
            pltpu.VMEM((2, slots // 2 * ROWS, LANES), f32),
            pltpu.VMEM((slots // 2, D), bf16),
            pltpu.VMEM((slots // 2, hidden), bf16),
            pltpu.SemaphoreType.DMA((13,)),
            one, one, eight, eight, eight, eight, one, one,
            one, one, one, four, one, one, one, one,
            one, two, one, one,
        ],
        compiler_params=pltpu.CompilerParams(
            collective_id=0, has_side_effects=True, vmem_limit_bytes=60 * 1024 * 1024
        ),
        name="layer",
    )(
        queries, keys, values, stream, norm_gain.reshape(1, D), out_weight, routes.T, gates.T,
        w_gate, w_up, w_down,
    )


def solution(mesh):
    placed = (
        P("ctx", "ep"),
        P("ctx", "ep"),
        P("ctx", None),
        P("ctx", None),
        P("ep", None),
        P(),
        P(("ctx", "ep"), None),
        P(("ctx", "ep"), None),
        P(("ctx", "ep"), None, None),
        P(("ctx", "ep"), None, None),
        P(("ctx", "ep"), None, None),
    )
    return jax.shard_map(
        local,
        mesh=mesh,
        in_specs=placed,
        out_specs=(P(("ctx", "ep"), None), P(("ctx", "ep"), None)),
        check_vma=False,
    )
```

```python
import functools

import jax
import jax.numpy as jnp
from jax import lax
from jax.experimental import pallas as pl
from jax.experimental.pallas import tpu as pltpu
from jax.sharding import PartitionSpec as P

D = 4096
HD = 128
TOP = 8
CAP = 3
ROWS = 16
COLS = D // ROWS
LANES = 128
MESH = pl.DeviceIdType.MESH
N_DEV = 128


def shifted(ctx, ep, j, sign):
    a, b, c = j % 4, (j // 4) % 4, (j // 16) % 4
    core = (ctx + j // 64) % 2
    z = (ctx // 2 + 4 + sign * ((a + b) % 4)) % 4
    y = ((ep % 2) * 2 + ctx // 8 + 4 + sign * ((a + 2 * b + c) % 4)) % 4
    x = (ep // 2 + 4 + sign * a) % 4
    return (y % 2) * 8 + z * 2 + core, x * 2 + y // 2


def offset_of(ctx, ep, to):
    core = (to >> 3) + ctx & 1
    z = (to >> 4) + 4 - ctx // 2 % 4 & 3
    y = ((to & 1) << 1) + (to >> 6) + 4 - (ep % 2 * 2 + ctx // 8) & 3
    a = (to >> 1 & 3) + 4 - ep // 2 & 3
    b = z + 4 - a & 3
    c = y + 12 - a - 2 * b & 3
    return core * 64 + c * 16 + b * 4 + a


def kv_peer(ctx, ep, o, sign):
    core = ctx % 2
    y = (ep % 2) * 2 + ctx // 8
    z = (ctx // 2 + 4 + sign * (o % 4)) % 4
    step = (o // 4) * (1 + 2 * core)
    y = (y + 4 + sign * step) % 4
    return (y % 2) * 8 + z * 2 + core, (ep // 2) * 2 + y // 2


def ep_peer(ep, o, sign):
    return ((ep // 2 + 4 + sign * (o // 2)) % 4) * 2 + (ep + o) % 2


def layer_kernel(
    q_hbm, k_hbm, v_hbm, stream_hbm, gain_hbm, ow_hbm, routes_hbm, gates_hbm, wg_hbm, wu_hbm, wd_hbm,
    resid_ref, out_ref,
    q_ref, stream_ref, gain_ref, ow, routes_ref, token_ref, place_ref, token_s, place_s, gate_s,
    kall, vall, score, qs, attn, part_out, along_in, flip_in, both_out, both_in, last_out, last_in, stream_in,
    wg, wu, wd, blocks, send, recv, ans, ret, wide, flat, hid,
    in_sem, k_send, v_send, k_recv, v_recv, k_sib, v_sib, st_send, st_recv,
    along_send, along_recv, flip_send, flip_recv, both_send, both_recv, last_send, last_recv,
    send_sem, recv_sem, ans_sem, ret_sem,
):
    ctx = lax.axis_index("ctx")
    ep = lax.axis_index("ep")
    rows = q_ref.shape[0]

    def block(c):
        return pl.ds(pl.multiple_of(c * rows, rows), rows)

    head = pl.ds(pl.multiple_of(ep // 2 * HD, HD), HD)
    pairs = (
        (k_hbm.at[:, head], kall.at[block(ctx)]),
        (v_hbm.at[:, head], vall.at[block(ctx)]),
        (routes_hbm, routes_ref),
        (gates_hbm, gate_s),
        (stream_hbm, stream_ref),
        (q_hbm, q_ref),
        (gain_hbm, gain_ref),
        (ow_hbm, ow),
        (wg_hbm.at[0], wg),
        (wu_hbm.at[0], wu),
        (wd_hbm.at[0], wd),
        (token_ref, token_s),
        (place_ref, place_s),
    )
    loads = [pltpu.make_async_copy(s, d, in_sem.at[i]) for i, (s, d) in enumerate(pairs)]
    for load in loads[:11]:
        load.start()
    sibling = (ctx // 2 * 2 + (ctx + 1) % 2, ep)
    barrier = pltpu.get_barrier_semaphore()
    for o in range(1, 5):
        pl.semaphore_signal(barrier, inc=1, device_id=kv_peer(ctx, ep, o, -1), device_id_type=MESH)
    for o in range(1, 8):
        pl.semaphore_signal(barrier, inc=1, device_id=(ctx, ep_peer(ep, o, -1)), device_id_type=MESH)
    pl.semaphore_signal(barrier, inc=1, device_id=sibling, device_id_type=MESH)

    loads[0].wait()
    loads[1].wait()
    pl.semaphore_wait(barrier, 12)

    def share(ref, c, send, recv, to):
        return pltpu.make_async_remote_copy(
            src_ref=ref.at[block(c)],
            dst_ref=ref.at[block(c)],
            send_sem=send,
            recv_sem=recv,
            device_id=to,
            device_id_type=MESH,
        )

    for o in (4, 1, 3, 2):
        to = kv_peer(ctx, ep, o, 1)
        share(kall, ctx, k_send, k_recv.at[o], to).start()
        share(vall, ctx, v_send, v_recv.at[o], to).start()
    share(kall, ctx, k_send, k_sib.at[0], sibling).start()
    share(vall, ctx, v_send, v_sib.at[0], sibling).start()
    loads[4].wait()
    stream_in[0] = stream_ref[pl.ds(pl.multiple_of(ep * 32, 32), 32), :]
    for o in range(1, 8):
        to = ep_peer(ep, o, 1)
        pltpu.make_async_remote_copy(
            src_ref=stream_ref.at[pl.ds(pl.multiple_of(to * 32, 32), 32)],
            dst_ref=stream_in.at[o],
            send_sem=st_send,
            recv_sem=st_recv,
            device_id=(ctx, to),
            device_id_type=MESH,
        ).start()

    def landed(ref, c, sem):
        part = ref.at[block(c)]
        pltpu.make_async_copy(part, part, sem).wait()

    loads[2].wait()
    shape = (N_DEV, 32)
    expert = lax.broadcasted_iota(jnp.int32, shape, 0)
    position = lax.broadcasted_iota(jnp.int32, shape, 1)
    named = [expert == routes_ref[k : k + 1, :] for k in range(TOP)]
    present = named[0]
    for k in range(1, TOP):
        present = present | named[k]
    left = jnp.where(present, position, 32)
    picks = []
    for s in range(CAP):
        picks.append(jnp.min(left, axis=1, keepdims=True))
        left = jnp.where(left > picks[s], left, 32)
    column = lax.broadcasted_iota(jnp.int32, (N_DEV, LANES), 1)
    table = jnp.where(column == 0, picks[0], jnp.where(column == 1, picks[1], picks[2]))
    token_ref[...] = jnp.where(table < 32, table, 0)
    rank = jnp.where(position > picks[0], 1, 0) + jnp.where(position > picks[1], 1, 0)
    slot = offset_of(ctx, ep, expert) * CAP + rank
    for k in range(TOP):
        place_ref[k : k + 1, 0:32] = jnp.sum(jnp.where(named[k], slot, 0), axis=0, keepdims=True)
    loads[11].start()
    loads[12].start()

    across = kv_peer(ctx, ep, 4, 1)
    for o in (1, 3, 4, 2, 5, 7, 6):
        c = kv_peer(ctx, ep, o, -1)[0]
        for ref, out_sem, at_sem, sib in ((kall, k_send, k_recv, k_sib), (vall, v_send, v_recv, v_sib)):
            landed(ref, c, at_sem.at[o])
            if o < 4:
                share(ref, c, out_sem, at_sem.at[o + 4], across).start()
            share(ref, c, out_sem, sib.at[o], sibling).start()
    for load in loads[5:8]:
        load.wait()
    for o in range(8):
        c = kv_peer(ctx, ep, o, -1)[0]
        other = c // 2 * 2 + (c + 1) % 2
        landed(kall, other, k_sib.at[o])
        landed(vall, other, v_sib.at[o])

    width = score.shape[2]
    factor = HD ** (-0.5) * 1.4426950408889634
    heads = q_ref.shape[1] // HD

    half_d = D // 2
    late = pl.ds(half_d, half_d)
    own_rows = pl.ds(pl.multiple_of(ep % 2 * 32, 32), 32)
    other_rows = pl.ds(pl.multiple_of((ep + 1) % 2 * 32, 32), 32)
    partner = ep_peer(ep, 1, 1)

    def landed_flip(dx):
        part = flip_in.at[dx]
        pltpu.make_async_copy(part, part, flip_recv.at[dx]).wait()

    def one_part(i, state):
        code, before = state
        dx = code % 4
        first = pl.multiple_of((ep // 2 + dx) % 4 * 64, 64)
        for h in range(heads):
            qs[64 * h : 64 * h + 64, :] = q_ref[pl.ds(first, 64), HD * h : HD * h + HD]
        last = (ctx * rows + first) // width
        lowest = jnp.full((64 * heads, LANES), -1e30, jnp.float32)
        zero = jnp.zeros((64 * heads, LANES), jnp.float32)

        def scores(t):
            keys = kall[pl.ds(pl.multiple_of(t * width, width), width), :]
            return lax.dot_general(
                qs[...], keys, (((1,), (1,)), ((), ())), preferred_element_type=jnp.float32
            )

        def look(t, top, masked=False):
            s = scores(t)
            if masked:
                query_pos = ctx * rows + first + lax.broadcasted_iota(jnp.int32, s.shape, 0) % 64
                key_pos = t * width + lax.broadcasted_iota(jnp.int32, s.shape, 1)
                s = jnp.where(key_pos <= query_pos, s, -1e30)
            score[t] = s
            for j in range(width // LANES):
                top = jnp.maximum(top, s[:, j * LANES : (j + 1) * LANES])
            return top

        def mix(t, state, top):
            total, mixed = state
            weight = jnp.exp2((score[t] - top) * factor)
            for j in range(width // LANES):
                total = total + weight[:, j * LANES : (j + 1) * LANES]
            mixed = mixed + jnp.dot(
                weight.astype(jnp.bfloat16),
                vall[pl.ds(pl.multiple_of(t * width, width), width), :],
                preferred_element_type=jnp.float32,
            )
            return total, mixed

        def finish(total, mixed):
            mixed = (mixed / jnp.sum(total, axis=1, keepdims=True)).astype(jnp.bfloat16)
            for h in range(heads):
                attn[:, HD * h : HD * h + HD] = mixed[64 * h : 64 * h + 64, :]

        tiles = score.shape[0]

        @pl.when(last == tiles - 1)
        def _():
            top = lowest
            for t in range(tiles):
                top = look(t, top, t == tiles - 1)
            top = jnp.max(top, axis=1, keepdims=True)
            state = zero, zero
            for t in range(tiles):
                state = mix(t, state, top)
            finish(*state)

        @pl.when(last < tiles - 1)
        def _():
            top = look(last, lax.fori_loop(0, last, look, lowest), True)
            top = jnp.max(top, axis=1, keepdims=True)
            finish(*lax.fori_loop(0, last + 1, functools.partial(mix, top=top), (zero, zero)))

        p = jnp.dot(attn[...], ow[...], preferred_element_type=jnp.float32).astype(jnp.bfloat16)
        part_out[dx] = p

        pltpu.make_async_remote_copy(
            src_ref=part_out.at[dx, other_rows, late],
            dst_ref=flip_in.at[dx],
            send_sem=flip_send,
            recv_sem=flip_recv.at[dx],
            device_id=(ctx, partner),
            device_id_type=MESH,
        ).start()

        @pl.when(dx > 0)
        def _():
            for n in range(2):
                cols = pl.ds(n * (half_d // 2), half_d // 2)
                pltpu.make_async_remote_copy(
                    src_ref=part_out.at[dx, :, cols],
                    dst_ref=along_in.at[dx, :, cols],
                    send_sem=along_send,
                    recv_sem=along_recv,
                    device_id=(ctx, ep_peer(ep, 2 * dx, 1)),
                    device_id_type=MESH,
                ).start()

        @pl.when(i > 0)
        def _():
            landed_flip(before)
            both = part_out[before, own_rows, late].astype(jnp.float32) + flip_in[before].astype(jnp.float32)
            both_out[before] = both.astype(jnp.bfloat16)
            pltpu.make_async_remote_copy(
                src_ref=both_out.at[before],
                dst_ref=both_in.at[before],
                send_sem=both_send,
                recv_sem=both_recv,
                device_id=(ctx, ep_peer(ep, 2 * before, 1)),
                device_id_type=MESH,
            ).start()

        return code // 4, dx

    lax.fori_loop(0, 4, one_part, (2 + 1 * 4 + 3 * 16 + 0 * 64, 0))

    def three_of(ref, sem):
        part = ref.at[pl.ds(1, 3)]
        pltpu.make_async_copy(part, part, sem).wait()

    three_of(along_in, along_recv)
    for n in range(4):
        cols = slice(n * 512, n * 512 + 512)
        total = part_out[0, other_rows, cols].astype(jnp.float32)
        for d in range(1, 4):
            total += along_in[d, other_rows, cols].astype(jnp.float32)
        last_out[:, cols] = total.astype(jnp.bfloat16)
    last = pltpu.make_async_remote_copy(
        src_ref=last_out,
        dst_ref=last_in,
        send_sem=last_send,
        recv_sem=last_recv,
        device_id=(ctx, partner),
        device_id_type=MESH,
    )
    last.start()

    def all_of(ref, sem):
        part = ref.at[pl.ds(1, 7)]
        pltpu.make_async_copy(part, part, sem).wait()

    all_of(stream_in, st_recv)
    landed_flip(0)
    three_of(both_in, both_recv)
    squares = jnp.zeros((32, LANES), jnp.float32)
    for g in (4, 5, 6, 7, 0, 1, 2, 3):
        cols = slice(512 * g, 512 * g + 512)
        if g == 0:
            last.wait_recv()
        total = part_out[0, own_rows, cols].astype(jnp.float32)
        if g < 4:
            total += last_in[:, cols].astype(jnp.float32)
            for d in range(1, 4):
                total += along_in[d, own_rows, cols].astype(jnp.float32)
        else:
            there = slice(512 * g - half_d, 512 * g - half_d + 512)
            total += flip_in[0, :, there].astype(jnp.float32)
            for d in range(1, 4):
                total += both_in[d, :, there].astype(jnp.float32)
        own = stream_in[(ep // 2 + 4 - g // 2) % 4 * 2 + (ep + g) % 2]
        total = (total + own.astype(jnp.float32)).astype(jnp.bfloat16)
        resid_ref[:, cols] = total
        total = total.astype(jnp.float32)
        for j in range(4):
            piece = total[:, j * LANES : (j + 1) * LANES]
            squares += piece * piece
    inverse = lax.rsqrt(jnp.sum(squares, axis=1, keepdims=True) / D + 1e-06)
    for r in range(ROWS):
        for h in range(2):
            at = r * COLS + h * LANES
            wide[h, pl.ds(r, 32, stride=ROWS), :] = (
                resid_ref[:, at : at + LANES].astype(jnp.float32) * inverse * gain_ref[:, at : at + LANES]
            )

    def store(t, carry):
        for h in range(2):
            blocks[t, :, h * LANES : (h + 1) * LANES] = wide[
                h, pl.ds(pl.multiple_of(t * ROWS, ROWS), ROWS), :
            ].astype(jnp.bfloat16)
        return carry

    lax.fori_loop(0, 32, store, 0)
    for i in (3, 11, 12):
        loads[i].wait()

    def pack(into, j, to_ctx, to_ep):
        to = to_ctx * 8 + to_ep
        for s in range(CAP):
            into[CAP * j + s] = blocks[token_s[to, s]]

    def dispatch(j, carry):
        to = shifted(ctx, ep, j, 1)
        pack(send, j, *to)
        pltpu.make_async_remote_copy(
            src_ref=send.at[pl.ds(CAP * j, CAP)],
            dst_ref=recv.at[pl.ds(CAP * j, CAP)],
            send_sem=send_sem,
            recv_sem=recv_sem.at[j // 64],
            device_id=to,
            device_id_type=MESH,
        ).start()
        return carry

    lax.fori_loop(1, N_DEV, dispatch, 0)
    pack(recv, 0, ctx, ep)

    half = N_DEV // 2
    count = half * CAP
    def one_chunk(chunk, carry):
        first = chunk * half

        def wait_for(begin, end, sem):
            arrived = recv.at[pl.ds(CAP * begin, CAP * (end - begin))]
            pltpu.make_async_copy(arrived, arrived, sem).wait()

        @pl.when(chunk == 0)
        def _():
            wait_for(1, half, recv_sem.at[0])

        @pl.when(chunk == 1)
        def _():
            wait_for(half, N_DEV, recv_sem.at[1])

        def flatten(i, carry):
            part = recv[pl.ds(CAP * first + 16 * i, 16)].reshape(16 * ROWS, COLS).astype(jnp.float32)
            for h in range(2):
                wide[h, pl.ds(0, 16 * ROWS), :] = part[:, h * LANES : (h + 1) * LANES]
            for r in range(ROWS):
                for h in range(2):
                    flat[pl.ds(16 * i, 16), r * COLS + h * LANES : r * COLS + (h + 1) * LANES] = wide[
                        h, pl.ds(r, 16, stride=ROWS), :
                    ].astype(jnp.bfloat16)
            return carry

        lax.fori_loop(0, count // 16, flatten, 0)

        @pl.when(chunk == 0)
        def _():
            for load in loads[8:11]:
                load.wait()

        g = jnp.dot(flat[...], wg[...], preferred_element_type=jnp.float32)
        u = jnp.dot(flat[...], wu[...], preferred_element_type=jnp.float32)
        hid[...] = (g / (1.0 + jnp.exp(-g)) * u).astype(jnp.bfloat16)

        def down(n, carry):
            cols = pl.ds(pl.multiple_of(n * 1024, 1024), 1024)
            o = jnp.dot(hid[...], wd[:, cols], preferred_element_type=jnp.float32)
            for r in range(4):
                for h in range(2):
                    at = r * COLS + h * LANES
                    wide[h, pl.ds(4 * n + r, count, stride=ROWS), :] = o[:, at : at + LANES]
            return carry

        lax.fori_loop(0, D // 1024, down, 0)

        def reply(into, at, i):
            for s in range(CAP):
                for h in range(2):
                    into[at + s, :, h * LANES : (h + 1) * LANES] = wide[
                        h, pl.ds(pl.multiple_of((CAP * i + s) * ROWS, ROWS), ROWS), :
                    ].astype(jnp.bfloat16)

        def send_back(i, carry):
            j = first + i
            reply(ans, CAP * j, i)
            pltpu.make_async_remote_copy(
                src_ref=ans.at[pl.ds(CAP * j, CAP)],
                dst_ref=ret.at[pl.ds(CAP * j, CAP)],
                send_sem=ans_sem,
                recv_sem=ret_sem,
                device_id=shifted(ctx, ep, j, -1),
                device_id_type=MESH,
            ).start()
            return carry

        @pl.when(chunk == 0)
        def _():
            reply(ret, 0, 0)

        lax.fori_loop(1 - chunk, half, send_back, 0)
        return carry

    lax.fori_loop(0, 2, one_chunk, 0)

    others = ret.at[pl.ds(CAP, CAP * (N_DEV - 1))]
    pltpu.make_async_copy(others, others, ret_sem).wait()

    def combine(t, carry):
        total = jnp.zeros((ROWS, COLS), jnp.float32)
        for k in range(TOP):
            total += gate_s[k, t] * ret[place_s[k, t]].astype(jnp.float32)
        for h in range(2):
            wide[h, pl.ds(pl.multiple_of(t * ROWS, ROWS), ROWS), :] = total[:, h * LANES : (h + 1) * LANES]
        return carry

    lax.fori_loop(0, 32, combine, 0)
    for r in range(ROWS):
        for h in range(2):
            out_ref[:, r * COLS + h * LANES : r * COLS + (h + 1) * LANES] = wide[
                h, pl.ds(r, 32, stride=ROWS), :
            ].astype(jnp.bfloat16)

    sent = send.at[pl.ds(CAP, CAP * (N_DEV - 1))]
    pltpu.make_async_copy(sent, sent, send_sem).wait()
    answered = ans.at[pl.ds(CAP, CAP * (N_DEV - 1))]
    pltpu.make_async_copy(answered, answered, ans_sem).wait()

    for ref, sem in ((kall, k_send), (vall, v_send)):
        gone = ref.at[pl.ds(0, 15 * rows)]
        pltpu.make_async_copy(gone, gone, sem).wait()
    all_of(stream_in, st_send)
    gone = flip_in
    pltpu.make_async_copy(gone, gone, flip_send).wait()
    three_of(along_in, along_send)
    three_of(both_out, both_send)
    last.wait_send()


def local(
    stream, queries, keys, values, out_weight, norm_gain, routes, gates, w_gate, w_up, w_down
):
    rows, width = queries.shape
    positions = rows * 16
    slots = N_DEV * CAP
    hidden = w_gate.shape[2]
    bf16, f32, i32 = jnp.bfloat16, jnp.float32, jnp.int32
    hbm = pl.BlockSpec(memory_space=pltpu.HBM)
    vmem = pl.BlockSpec(memory_space=pltpu.VMEM)
    one = pltpu.SemaphoreType.DMA
    two = pltpu.SemaphoreType.DMA((2,))
    four = pltpu.SemaphoreType.DMA((4,))
    eight = pltpu.SemaphoreType.DMA((8,))
    box = pltpu.VMEM((slots, ROWS, COLS), bf16)
    return pl.pallas_call(
        layer_kernel,
        out_shape=(pltpu.VMEM((32, D), bf16), pltpu.VMEM((32, D), bf16)),
        in_specs=[hbm] * 11,
        out_specs=(vmem, vmem),
        scratch_shapes=[
            pltpu.VMEM(queries.shape, bf16),
            pltpu.VMEM(stream.shape, bf16),
            pltpu.VMEM((1, D), f32),
            pltpu.VMEM(out_weight.shape, bf16),
            pltpu.VMEM((TOP, 32), i32),
            pltpu.VMEM((N_DEV, LANES), i32),
            pltpu.VMEM((TOP, LANES), i32),
            pltpu.SMEM((N_DEV, LANES), i32),
            pltpu.SMEM((TOP, LANES), i32),
            pltpu.SMEM((TOP, 32), f32),
            pltpu.VMEM((positions, HD), bf16),
            pltpu.VMEM((positions, HD), bf16),
            pltpu.VMEM((positions // 1024, width // HD * 64, 1024), f32),
            pltpu.VMEM((width // HD * 64, HD), bf16),
            pltpu.VMEM((64, width), bf16),
            pltpu.VMEM((4, 64, D), bf16),
            pltpu.VMEM((4, 64, D // 2), bf16),
            pltpu.VMEM((4, 32, D // 2), bf16),
            pltpu.VMEM((4, 32, D // 2), bf16),
            pltpu.VMEM((4, 32, D // 2), bf16),
            pltpu.VMEM((32, D // 2), bf16),
            pltpu.VMEM((32, D // 2), bf16),
            pltpu.VMEM((8, 32, D // 8), bf16),
            pltpu.VMEM((D, hidden), bf16),
            pltpu.VMEM((D, hidden), bf16),
            pltpu.VMEM((hidden, D), bf16),
            pltpu.VMEM((32, ROWS, COLS), bf16),
            box, box, box, box,
            pltpu.VMEM((2, slots // 2 * ROWS, LANES), f32),
            pltpu.VMEM((slots // 2, D), bf16),
            pltpu.VMEM((slots // 2, hidden), bf16),
            pltpu.SemaphoreType.DMA((13,)),
            one, one, eight, eight, eight, eight, one, one,
            one, one, one, four, one, one, one, one,
            one, two, one, one,
        ],
        compiler_params=pltpu.CompilerParams(
            collective_id=0, has_side_effects=True, vmem_limit_bytes=60 * 1024 * 1024
        ),
        name="layer",
    )(
        queries, keys, values, stream, norm_gain.reshape(1, D), out_weight, routes.T, gates.T,
        w_gate, w_up, w_down,
    )


def solution(mesh):
    placed = (
        P("ctx", "ep"),
        P("ctx", "ep"),
        P("ctx", None),
        P("ctx", None),
        P("ep", None),
        P(),
        P(("ctx", "ep"), None),
        P(("ctx", "ep"), None),
        P(("ctx", "ep"), None, None),
        P(("ctx", "ep"), None, None),
        P(("ctx", "ep"), None, None),
    )
    return jax.shard_map(
        local,
        mesh=mesh,
        in_specs=placed,
        out_specs=(P(("ctx", "ep"), None), P(("ctx", "ep"), None)),
        check_vma=False,
    )
```

```python
import functools

import jax
import jax.numpy as jnp
from jax import lax
from jax.experimental import pallas as pl
from jax.experimental.pallas import tpu as pltpu
from jax.sharding import PartitionSpec as P

D = 4096
HD = 128
TOP = 8
CAP = 3
ROWS = 16
COLS = D // ROWS
LANES = 128
MESH = pl.DeviceIdType.MESH
N_DEV = 128


def shifted(ctx, ep, j, sign):
    a, b, c = j % 4, (j // 4) % 4, (j // 16) % 4
    core = (ctx + j // 64) % 2
    z = (ctx // 2 + 4 + sign * ((a + b) % 4)) % 4
    y = ((ep % 2) * 2 + ctx // 8 + 4 + sign * ((2 * a + b + c) % 4)) % 4
    x = (ep // 2 + 4 + sign * a) % 4
    return (y % 2) * 8 + z * 2 + core, x * 2 + y // 2


def offset_of(ctx, ep, to):
    core = (to >> 3) + ctx & 1
    z = (to >> 4) + 4 - ctx // 2 % 4 & 3
    y = ((to & 1) << 1) + (to >> 6) + 4 - (ep % 2 * 2 + ctx // 8) & 3
    a = (to >> 1 & 3) + 4 - ep // 2 & 3
    b = z + 4 - a & 3
    c = y + 12 - 2 * a - b & 3
    return core * 64 + c * 16 + b * 4 + a


def kv_peer(ctx, ep, o, sign):
    core = ctx % 2
    y = (ep % 2) * 2 + ctx // 8
    z = (ctx // 2 + 4 + sign * (o % 4)) % 4
    step = (o // 4) * (1 + 2 * core)
    y = (y + 4 + sign * step) % 4
    return (y % 2) * 8 + z * 2 + core, (ep // 2) * 2 + y // 2


def ep_peer(ep, o, sign):
    return ((ep // 2 + 4 + sign * (o // 2)) % 4) * 2 + (ep + o) % 2


def layer_kernel(
    q_hbm, k_hbm, v_hbm, stream_hbm, gain_hbm, ow_hbm, routes_hbm, gates_hbm, wg_hbm, wu_hbm, wd_hbm,
    resid_ref, out_ref,
    q_ref, stream_ref, gain_ref, ow, routes_ref, token_ref, place_ref, token_s, place_s, gate_s,
    kall, vall, score, qs, attn, part_out, along_in, flip_in, both_out, both_in, last_out, last_in, stream_in,
    wg, wu, wd, blocks, send, recv, ans, ret, wide, flat, hid,
    in_sem, k_send, v_send, k_recv, v_recv, k_sib, v_sib, st_send, st_recv,
    along_send, along_recv, flip_send, flip_recv, both_send, both_recv, last_send, last_recv,
    send_sem, recv_sem, ans_sem, ret_sem,
):
    ctx = lax.axis_index("ctx")
    ep = lax.axis_index("ep")
    rows = q_ref.shape[0]

    def block(c):
        return pl.ds(pl.multiple_of(c * rows, rows), rows)

    head = pl.ds(pl.multiple_of(ep // 2 * HD, HD), HD)
    pairs = (
        (k_hbm.at[:, head], kall.at[block(ctx)]),
        (v_hbm.at[:, head], vall.at[block(ctx)]),
        (routes_hbm, routes_ref),
        (gates_hbm, gate_s),
        (stream_hbm, stream_ref),
        (q_hbm, q_ref),
        (gain_hbm, gain_ref),
        (ow_hbm, ow),
        (wg_hbm.at[0], wg),
        (wu_hbm.at[0], wu),
        (wd_hbm.at[0], wd),
        (token_ref, token_s),
        (place_ref, place_s),
    )
    loads = [pltpu.make_async_copy(s, d, in_sem.at[i]) for i, (s, d) in enumerate(pairs)]
    for load in loads[:11]:
        load.start()
    sibling = (ctx // 2 * 2 + (ctx + 1) % 2, ep)
    barrier = pltpu.get_barrier_semaphore()
    for o in range(1, 5):
        pl.semaphore_signal(barrier, inc=1, device_id=kv_peer(ctx, ep, o, -1), device_id_type=MESH)
    for o in range(1, 8):
        pl.semaphore_signal(barrier, inc=1, device_id=(ctx, ep_peer(ep, o, -1)), device_id_type=MESH)
    pl.semaphore_signal(barrier, inc=1, device_id=sibling, device_id_type=MESH)

    loads[0].wait()
    loads[1].wait()
    pl.semaphore_wait(barrier, 12)

    def share(ref, c, send, recv, to):
        return pltpu.make_async_remote_copy(
            src_ref=ref.at[block(c)],
            dst_ref=ref.at[block(c)],
            send_sem=send,
            recv_sem=recv,
            device_id=to,
            device_id_type=MESH,
        )

    for o in (4, 1, 3, 2):
        to = kv_peer(ctx, ep, o, 1)
        share(kall, ctx, k_send, k_recv.at[o], to).start()
        share(vall, ctx, v_send, v_recv.at[o], to).start()
    share(kall, ctx, k_send, k_sib.at[0], sibling).start()
    share(vall, ctx, v_send, v_sib.at[0], sibling).start()
    loads[4].wait()
    stream_in[0] = stream_ref[pl.ds(pl.multiple_of(ep * 32, 32), 32), :]
    for o in range(1, 8):
        to = ep_peer(ep, o, 1)
        pltpu.make_async_remote_copy(
            src_ref=stream_ref.at[pl.ds(pl.multiple_of(to * 32, 32), 32)],
            dst_ref=stream_in.at[o],
            send_sem=st_send,
            recv_sem=st_recv,
            device_id=(ctx, to),
            device_id_type=MESH,
        ).start()

    def landed(ref, c, sem):
        part = ref.at[block(c)]
        pltpu.make_async_copy(part, part, sem).wait()

    loads[2].wait()
    shape = (N_DEV, 32)
    expert = lax.broadcasted_iota(jnp.int32, shape, 0)
    position = lax.broadcasted_iota(jnp.int32, shape, 1)
    named = [expert == routes_ref[k : k + 1, :] for k in range(TOP)]
    present = named[0]
    for k in range(1, TOP):
        present = present | named[k]
    left = jnp.where(present, position, 32)
    picks = []
    for s in range(CAP):
        picks.append(jnp.min(left, axis=1, keepdims=True))
        left = jnp.where(left > picks[s], left, 32)
    column = lax.broadcasted_iota(jnp.int32, (N_DEV, LANES), 1)
    table = jnp.where(column == 0, picks[0], jnp.where(column == 1, picks[1], picks[2]))
    token_ref[...] = jnp.where(table < 32, table, 0)
    rank = jnp.where(position > picks[0], 1, 0) + jnp.where(position > picks[1], 1, 0)
    slot = offset_of(ctx, ep, expert) * CAP + rank
    for k in range(TOP):
        place_ref[k : k + 1, 0:32] = jnp.sum(jnp.where(named[k], slot, 0), axis=0, keepdims=True)
    loads[11].start()
    loads[12].start()

    across = kv_peer(ctx, ep, 4, 1)
    for o in (1, 3, 4, 2, 5, 7, 6):
        c = kv_peer(ctx, ep, o, -1)[0]
        for ref, out_sem, at_sem, sib in ((kall, k_send, k_recv, k_sib), (vall, v_send, v_recv, v_sib)):
            landed(ref, c, at_sem.at[o])
            if o < 4:
                share(ref, c, out_sem, at_sem.at[o + 4], across).start()
            share(ref, c, out_sem, sib.at[o], sibling).start()
    for load in loads[5:8]:
        load.wait()
    for o in range(8):
        c = kv_peer(ctx, ep, o, -1)[0]
        other = c // 2 * 2 + (c + 1) % 2
        landed(kall, other, k_sib.at[o])
        landed(vall, other, v_sib.at[o])

    width = score.shape[2]
    factor = HD ** (-0.5) * 1.4426950408889634
    heads = q_ref.shape[1] // HD

    half_d = D // 2
    late = pl.ds(half_d, half_d)
    own_rows = pl.ds(pl.multiple_of(ep % 2 * 32, 32), 32)
    other_rows = pl.ds(pl.multiple_of((ep + 1) % 2 * 32, 32), 32)
    partner = ep_peer(ep, 1, 1)

    def landed_flip(dx):
        part = flip_in.at[dx]
        pltpu.make_async_copy(part, part, flip_recv.at[dx]).wait()

    def one_part(i, state):
        code, before = state
        dx = code % 4
        first = pl.multiple_of((ep // 2 + dx) % 4 * 64, 64)
        for h in range(heads):
            qs[64 * h : 64 * h + 64, :] = q_ref[pl.ds(first, 64), HD * h : HD * h + HD]
        last = (ctx * rows + first) // width
        lowest = jnp.full((64 * heads, LANES), -1e30, jnp.float32)
        zero = jnp.zeros((64 * heads, LANES), jnp.float32)

        def scores(t):
            keys = kall[pl.ds(pl.multiple_of(t * width, width), width), :]
            return lax.dot_general(
                qs[...], keys, (((1,), (1,)), ((), ())), preferred_element_type=jnp.float32
            )

        def look(t, top, masked=False):
            s = scores(t)
            if masked:
                query_pos = ctx * rows + first + lax.broadcasted_iota(jnp.int32, s.shape, 0) % 64
                key_pos = t * width + lax.broadcasted_iota(jnp.int32, s.shape, 1)
                s = jnp.where(key_pos <= query_pos, s, -1e30)
            score[t] = s
            for j in range(width // LANES):
                top = jnp.maximum(top, s[:, j * LANES : (j + 1) * LANES])
            return top

        def mix(t, state, top):
            total, mixed = state
            weight = jnp.exp2((score[t] - top) * factor)
            for j in range(width // LANES):
                total = total + weight[:, j * LANES : (j + 1) * LANES]
            mixed = mixed + jnp.dot(
                weight.astype(jnp.bfloat16),
                vall[pl.ds(pl.multiple_of(t * width, width), width), :],
                preferred_element_type=jnp.float32,
            )
            return total, mixed

        def finish(total, mixed):
            mixed = (mixed / jnp.sum(total, axis=1, keepdims=True)).astype(jnp.bfloat16)
            for h in range(heads):
                attn[:, HD * h : HD * h + HD] = mixed[64 * h : 64 * h + 64, :]

        tiles = score.shape[0]

        @pl.when(last == tiles - 1)
        def _():
            top = lowest
            for t in range(tiles):
                top = look(t, top, t == tiles - 1)
            top = jnp.max(top, axis=1, keepdims=True)
            state = zero, zero
            for t in range(tiles):
                state = mix(t, state, top)
            finish(*state)

        @pl.when(last < tiles - 1)
        def _():
            top = look(last, lax.fori_loop(0, last, look, lowest), True)
            top = jnp.max(top, axis=1, keepdims=True)
            finish(*lax.fori_loop(0, last + 1, functools.partial(mix, top=top), (zero, zero)))

        p = jnp.dot(attn[...], ow[...], preferred_element_type=jnp.float32).astype(jnp.bfloat16)
        part_out[dx] = p

        pltpu.make_async_remote_copy(
            src_ref=part_out.at[dx, other_rows, late],
            dst_ref=flip_in.at[dx],
            send_sem=flip_send,
            recv_sem=flip_recv.at[dx],
            device_id=(ctx, partner),
            device_id_type=MESH,
        ).start()

        @pl.when(dx > 0)
        def _():
            for n in range(2):
                cols = pl.ds(n * (half_d // 2), half_d // 2)
                pltpu.make_async_remote_copy(
                    src_ref=part_out.at[dx, :, cols],
                    dst_ref=along_in.at[dx, :, cols],
                    send_sem=along_send,
                    recv_sem=along_recv,
                    device_id=(ctx, ep_peer(ep, 2 * dx, 1)),
                    device_id_type=MESH,
                ).start()

        @pl.when(i > 0)
        def _():
            landed_flip(before)
            both = part_out[before, own_rows, late].astype(jnp.float32) + flip_in[before].astype(jnp.float32)
            both_out[before] = both.astype(jnp.bfloat16)
            pltpu.make_async_remote_copy(
                src_ref=both_out.at[before],
                dst_ref=both_in.at[before],
                send_sem=both_send,
                recv_sem=both_recv,
                device_id=(ctx, ep_peer(ep, 2 * before, 1)),
                device_id_type=MESH,
            ).start()

        return code // 4, dx

    lax.fori_loop(0, 4, one_part, (2 + 1 * 4 + 3 * 16 + 0 * 64, 0))

    def three_of(ref, sem):
        part = ref.at[pl.ds(1, 3)]
        pltpu.make_async_copy(part, part, sem).wait()

    three_of(along_in, along_recv)
    for n in range(4):
        cols = slice(n * 512, n * 512 + 512)
        total = part_out[0, other_rows, cols].astype(jnp.float32)
        for d in range(1, 4):
            total += along_in[d, other_rows, cols].astype(jnp.float32)
        last_out[:, cols] = total.astype(jnp.bfloat16)
    last = pltpu.make_async_remote_copy(
        src_ref=last_out,
        dst_ref=last_in,
        send_sem=last_send,
        recv_sem=last_recv,
        device_id=(ctx, partner),
        device_id_type=MESH,
    )
    last.start()

    def all_of(ref, sem):
        part = ref.at[pl.ds(1, 7)]
        pltpu.make_async_copy(part, part, sem).wait()

    all_of(stream_in, st_recv)
    landed_flip(0)
    three_of(both_in, both_recv)
    squares = jnp.zeros((32, LANES), jnp.float32)
    for g in (4, 5, 6, 7, 0, 1, 2, 3):
        cols = slice(512 * g, 512 * g + 512)
        if g == 0:
            last.wait_recv()
        total = part_out[0, own_rows, cols].astype(jnp.float32)
        if g < 4:
            total += last_in[:, cols].astype(jnp.float32)
            for d in range(1, 4):
                total += along_in[d, own_rows, cols].astype(jnp.float32)
        else:
            there = slice(512 * g - half_d, 512 * g - half_d + 512)
            total += flip_in[0, :, there].astype(jnp.float32)
            for d in range(1, 4):
                total += both_in[d, :, there].astype(jnp.float32)
        own = stream_in[(ep // 2 + 4 - g // 2) % 4 * 2 + (ep + g) % 2]
        total = (total + own.astype(jnp.float32)).astype(jnp.bfloat16)
        resid_ref[:, cols] = total
        total = total.astype(jnp.float32)
        for j in range(4):
            piece = total[:, j * LANES : (j + 1) * LANES]
            squares += piece * piece
    inverse = lax.rsqrt(jnp.sum(squares, axis=1, keepdims=True) / D + 1e-06)
    for r in range(ROWS):
        for h in range(2):
            at = r * COLS + h * LANES
            wide[h, pl.ds(r, 32, stride=ROWS), :] = (
                resid_ref[:, at : at + LANES].astype(jnp.float32) * inverse * gain_ref[:, at : at + LANES]
            )

    def store(t, carry):
        for h in range(2):
            blocks[t, :, h * LANES : (h + 1) * LANES] = wide[
                h, pl.ds(pl.multiple_of(t * ROWS, ROWS), ROWS), :
            ].astype(jnp.bfloat16)
        return carry

    lax.fori_loop(0, 32, store, 0)
    for i in (3, 11, 12):
        loads[i].wait()

    def pack(into, j, to_ctx, to_ep):
        to = to_ctx * 8 + to_ep
        for s in range(CAP):
            into[CAP * j + s] = blocks[token_s[to, s]]

    def dispatch(j, carry):
        to = shifted(ctx, ep, j, 1)
        pack(send, j, *to)
        pltpu.make_async_remote_copy(
            src_ref=send.at[pl.ds(CAP * j, CAP)],
            dst_ref=recv.at[pl.ds(CAP * j, CAP)],
            send_sem=send_sem,
            recv_sem=recv_sem.at[j // 64],
            device_id=to,
            device_id_type=MESH,
        ).start()
        return carry

    lax.fori_loop(1, N_DEV, dispatch, 0)
    pack(recv, 0, ctx, ep)

    half = N_DEV // 2
    count = half * CAP
    def one_chunk(chunk, carry):
        first = chunk * half

        def wait_for(begin, end, sem):
            arrived = recv.at[pl.ds(CAP * begin, CAP * (end - begin))]
            pltpu.make_async_copy(arrived, arrived, sem).wait()

        @pl.when(chunk == 0)
        def _():
            wait_for(1, half, recv_sem.at[0])

        @pl.when(chunk == 1)
        def _():
            wait_for(half, N_DEV, recv_sem.at[1])

        def flatten(i, carry):
            part = recv[pl.ds(CAP * first + 16 * i, 16)].reshape(16 * ROWS, COLS).astype(jnp.float32)
            for h in range(2):
                wide[h, pl.ds(0, 16 * ROWS), :] = part[:, h * LANES : (h + 1) * LANES]
            for r in range(ROWS):
                for h in range(2):
                    flat[pl.ds(16 * i, 16), r * COLS + h * LANES : r * COLS + (h + 1) * LANES] = wide[
                        h, pl.ds(r, 16, stride=ROWS), :
                    ].astype(jnp.bfloat16)
            return carry

        lax.fori_loop(0, count // 16, flatten, 0)

        @pl.when(chunk == 0)
        def _():
            for load in loads[8:11]:
                load.wait()

        g = jnp.dot(flat[...], wg[...], preferred_element_type=jnp.float32)
        u = jnp.dot(flat[...], wu[...], preferred_element_type=jnp.float32)
        hid[...] = (g / (1.0 + jnp.exp(-g)) * u).astype(jnp.bfloat16)

        def down(n, carry):
            cols = pl.ds(pl.multiple_of(n * 1024, 1024), 1024)
            o = jnp.dot(hid[...], wd[:, cols], preferred_element_type=jnp.float32)
            for r in range(4):
                for h in range(2):
                    at = r * COLS + h * LANES
                    wide[h, pl.ds(4 * n + r, count, stride=ROWS), :] = o[:, at : at + LANES]
            return carry

        lax.fori_loop(0, D // 1024, down, 0)

        def reply(into, at, i):
            for s in range(CAP):
                for h in range(2):
                    into[at + s, :, h * LANES : (h + 1) * LANES] = wide[
                        h, pl.ds(pl.multiple_of((CAP * i + s) * ROWS, ROWS), ROWS), :
                    ].astype(jnp.bfloat16)

        def send_back(i, carry):
            j = first + i
            reply(ans, CAP * j, i)
            pltpu.make_async_remote_copy(
                src_ref=ans.at[pl.ds(CAP * j, CAP)],
                dst_ref=ret.at[pl.ds(CAP * j, CAP)],
                send_sem=ans_sem,
                recv_sem=ret_sem,
                device_id=shifted(ctx, ep, j, -1),
                device_id_type=MESH,
            ).start()
            return carry

        @pl.when(chunk == 0)
        def _():
            reply(ret, 0, 0)

        lax.fori_loop(1 - chunk, half, send_back, 0)
        return carry

    lax.fori_loop(0, 2, one_chunk, 0)

    others = ret.at[pl.ds(CAP, CAP * (N_DEV - 1))]
    pltpu.make_async_copy(others, others, ret_sem).wait()

    def combine(t, carry):
        total = jnp.zeros((ROWS, COLS), jnp.float32)
        for k in range(TOP):
            total += gate_s[k, t] * ret[place_s[k, t]].astype(jnp.float32)
        for h in range(2):
            wide[h, pl.ds(pl.multiple_of(t * ROWS, ROWS), ROWS), :] = total[:, h * LANES : (h + 1) * LANES]
        return carry

    lax.fori_loop(0, 32, combine, 0)
    for r in range(ROWS):
        for h in range(2):
            out_ref[:, r * COLS + h * LANES : r * COLS + (h + 1) * LANES] = wide[
                h, pl.ds(r, 32, stride=ROWS), :
            ].astype(jnp.bfloat16)

    sent = send.at[pl.ds(CAP, CAP * (N_DEV - 1))]
    pltpu.make_async_copy(sent, sent, send_sem).wait()
    answered = ans.at[pl.ds(CAP, CAP * (N_DEV - 1))]
    pltpu.make_async_copy(answered, answered, ans_sem).wait()

    for ref, sem in ((kall, k_send), (vall, v_send)):
        gone = ref.at[pl.ds(0, 15 * rows)]
        pltpu.make_async_copy(gone, gone, sem).wait()
    all_of(stream_in, st_send)
    gone = flip_in
    pltpu.make_async_copy(gone, gone, flip_send).wait()
    three_of(along_in, along_send)
    three_of(both_out, both_send)
    last.wait_send()


def local(
    stream, queries, keys, values, out_weight, norm_gain, routes, gates, w_gate, w_up, w_down
):
    rows, width = queries.shape
    positions = rows * 16
    slots = N_DEV * CAP
    hidden = w_gate.shape[2]
    bf16, f32, i32 = jnp.bfloat16, jnp.float32, jnp.int32
    hbm = pl.BlockSpec(memory_space=pltpu.HBM)
    vmem = pl.BlockSpec(memory_space=pltpu.VMEM)
    one = pltpu.SemaphoreType.DMA
    two = pltpu.SemaphoreType.DMA((2,))
    four = pltpu.SemaphoreType.DMA((4,))
    eight = pltpu.SemaphoreType.DMA((8,))
    box = pltpu.VMEM((slots, ROWS, COLS), bf16)
    return pl.pallas_call(
        layer_kernel,
        out_shape=(pltpu.VMEM((32, D), bf16), pltpu.VMEM((32, D), bf16)),
        in_specs=[hbm] * 11,
        out_specs=(vmem, vmem),
        scratch_shapes=[
            pltpu.VMEM(queries.shape, bf16),
            pltpu.VMEM(stream.shape, bf16),
            pltpu.VMEM((1, D), f32),
            pltpu.VMEM(out_weight.shape, bf16),
            pltpu.VMEM((TOP, 32), i32),
            pltpu.VMEM((N_DEV, LANES), i32),
            pltpu.VMEM((TOP, LANES), i32),
            pltpu.SMEM((N_DEV, LANES), i32),
            pltpu.SMEM((TOP, LANES), i32),
            pltpu.SMEM((TOP, 32), f32),
            pltpu.VMEM((positions, HD), bf16),
            pltpu.VMEM((positions, HD), bf16),
            pltpu.VMEM((positions // 1024, width // HD * 64, 1024), f32),
            pltpu.VMEM((width // HD * 64, HD), bf16),
            pltpu.VMEM((64, width), bf16),
            pltpu.VMEM((4, 64, D), bf16),
            pltpu.VMEM((4, 64, D // 2), bf16),
            pltpu.VMEM((4, 32, D // 2), bf16),
            pltpu.VMEM((4, 32, D // 2), bf16),
            pltpu.VMEM((4, 32, D // 2), bf16),
            pltpu.VMEM((32, D // 2), bf16),
            pltpu.VMEM((32, D // 2), bf16),
            pltpu.VMEM((8, 32, D // 8), bf16),
            pltpu.VMEM((D, hidden), bf16),
            pltpu.VMEM((D, hidden), bf16),
            pltpu.VMEM((hidden, D), bf16),
            pltpu.VMEM((32, ROWS, COLS), bf16),
            box, box, box, box,
            pltpu.VMEM((2, slots // 2 * ROWS, LANES), f32),
            pltpu.VMEM((slots // 2, D), bf16),
            pltpu.VMEM((slots // 2, hidden), bf16),
            pltpu.SemaphoreType.DMA((13,)),
            one, one, eight, eight, eight, eight, one, one,
            one, one, one, four, one, one, one, one,
            one, two, one, one,
        ],
        compiler_params=pltpu.CompilerParams(
            collective_id=0, has_side_effects=True, vmem_limit_bytes=60 * 1024 * 1024
        ),
        name="layer",
    )(
        queries, keys, values, stream, norm_gain.reshape(1, D), out_weight, routes.T, gates.T,
        w_gate, w_up, w_down,
    )


def solution(mesh):
    placed = (
        P("ctx", "ep"),
        P("ctx", "ep"),
        P("ctx", None),
        P("ctx", None),
        P("ep", None),
        P(),
        P(("ctx", "ep"), None),
        P(("ctx", "ep"), None),
        P(("ctx", "ep"), None, None),
        P(("ctx", "ep"), None, None),
        P(("ctx", "ep"), None, None),
    )
    return jax.shard_map(
        local,
        mesh=mesh,
        in_specs=placed,
        out_specs=(P(("ctx", "ep"), None), P(("ctx", "ep"), None)),
        check_vma=False,
    )
```
